32 devices in a mesh: groups: 2 (over y), tensor: 8 (over z, x), dp: 2 (over core).
Axes of the slice: x: 2, y: 2, z: 4, core: 2. Of those that a mesh axis runs over, the one named last changes fastest.
Arguments:
- tokens: bfloat16 [512, 8192], P(('groups', 'dp'), 'tensor'), parts along dimension 0, may hold values from -6 to 6
- cotangent: bfloat16 [512, 8192], P(('groups', 'dp'), 'tensor'), parts along dimension 0, may hold values from -6 to 6
- fwd_values: bfloat16 [16, 56, 128, 128], P(('groups', 'tensor')), parts along dimension 0, may hold values from -0.15625 to 0.15625
- fwd_ids: int32 [16, 56], P(('groups', 'tensor')), parts along dimension 0, may hold values from 0 to 191, as said below
- fwd_count: int32 [16], P(('groups', 'tensor')), parts along dimension 0, may hold values from 14 to 56
- bwd_ids: int32 [16, 96], P(('groups', 'tensor')), parts along dimension 0, may hold values from 0 to 191, as said below
- bwd_count: int32 [16], P(('groups', 'tensor')), parts along dimension 0, may hold values from 34 to 96, as said below
Outputs:
- input_grad: bfloat16 [512, 8192], P(('groups', 'dp'), 'tensor'), parts along dimension 0
- tile_grads: bfloat16 [16, 96, 128, 128], P(('groups', 'tensor')), parts along dimension 0
The draws below stay inside these ranges and needn't reach their ends.
There are 2 independent parts, one for each index of `groups`. The reference program is written for one: setup_inputs(seed, part) draws one part's arguments, and reference() takes and returns one part's arrays. A program takes and returns all parts, laid end to end along the dimension named above; each array names one. Nothing has to cross between parts.
Inputs may be any that keep to these rules, and one draw needn't show every extreme that they name: `fwd_ids`: each row holds distinct numbers; e names the tile of kind e // 64 (gate, up, down) at feature block e % 64 of the owner's hidden block. Only the first fwd_count entries of a row are live. `bwd_ids`: each row holds distinct numbers, coded as in fwd_ids; the first fwd_count[o] entries of row o equal those of fwd_ids. Only the first bwd_count entries of a row are live. `bwd_count`: at least fwd_count of the same owner.
All inputs are finite; a program needn't handle non-finite values.
Results may differ from the reference program's by a relative error of at most 0.0059.
Values may be sent and summed in bfloat16 or wider, within the bound.
No kernel may reach another device: no remote copies, remote signals or barrier semaphores. Data moves between devices by JAX's collectives and lax.ppermute only.
A program may use at most 64 MiB of HBM per device.

```python
import jax
import jax.numpy as jnp
from jax import lax

D = 8192
BLK = 128
TOK_DP = 128
FCAP = 56
BCAP = 96
OWNERS = 8
DBLK = 64
TOKENS = 256
N_TENSOR = 8
N_DP = 2


def owner_sets(key):
    sub_keys = jax.random.split(key, OWNERS)
    orders = jax.vmap(lambda sub_key: jax.random.permutation(sub_key, 3 * (D // BLK)))(sub_keys)
    return orders.astype(jnp.int32)


def owner_counts(key):
    key_a, key_b, key_c, key_d = jax.random.split(jax.random.fold_in(key, 11), 4)
    forward_n = jax.random.randint(key_a, (OWNERS,), FCAP // 4, FCAP + 1)
    top_fwd = jax.random.randint(key_b, (), 0, OWNERS)
    forward_n = forward_n.at[top_fwd].set(FCAP)
    extra_n = jax.random.randint(key_c, (OWNERS,), (BCAP - FCAP) // 2, BCAP - FCAP + 1)
    backward_n = jnp.minimum(forward_n + extra_n, BCAP)
    top_bwd = jax.random.randint(key_d, (), 0, OWNERS)
    backward_n = backward_n.at[top_bwd].set(BCAP)
    return (forward_n.astype(jnp.int32), backward_n.astype(jnp.int32))


def draw_fwd_ids(key, part):
    orders = owner_sets(key)
    return orders[:, :FCAP]


def draw_bwd_ids(key, part):
    orders = owner_sets(key)
    return orders[:, :BCAP]


def draw_fwd_count(key, part):
    forward_n, backward_n = owner_counts(key)
    return forward_n


def draw_bwd_count(key, part):
    forward_n, backward_n = owner_counts(key)
    return backward_n


def level_of(rng, extent, shards, smallest, largest):
    gain, own = 1.0, jax.random.fold_in(rng, 6)
    for position, parts in shards:
        draws = jnp.exp(jax.random.uniform(jax.random.fold_in(own, position), (parts,), jnp.float32, smallest / len(shards), largest / len(shards)))
        gain = gain * jnp.repeat(draws, extent[position] // parts).reshape([-1 if axis == position else 1 for axis in range(len(extent))])
    return gain


def gaussian(rng, shape, width, bound, cuts=(), held_as=jnp.bfloat16):
    result = width * jax.random.normal(rng, shape, jnp.float32)
    if cuts:
        result = result * level_of(rng, shape, cuts, -0.22, 0.18)
    return jnp.clip(result, -bound, bound).astype(held_as)


def setup_inputs(seed: int = 0, part: int = 0) -> dict:
    keys = jax.random.split(jax.random.key(seed), 8)
    own_keys = jax.random.split(jax.random.fold_in(keys[7], part), 8)
    return {
        "tokens": gaussian(own_keys[0], (TOKENS, D), 1.0, 6.0, ((0, 2), (1, 8))),
        "cotangent": gaussian(own_keys[1], (TOKENS, D), 1.0, 6.0, ((0, 2), (1, 8))),
        "fwd_values": gaussian(own_keys[2], (OWNERS, FCAP, BLK, BLK), (BLK * DBLK // 5) ** -0.5, 0.15625, ((0, 8),)),
        "fwd_ids": draw_fwd_ids(jax.random.fold_in(jax.random.fold_in(keys[7], part), 71), part),
        "fwd_count": draw_fwd_count(jax.random.fold_in(jax.random.fold_in(keys[7], part), 71), part),
        "bwd_ids": draw_bwd_ids(jax.random.fold_in(jax.random.fold_in(keys[7], part), 71), part),
        "bwd_count": draw_bwd_count(jax.random.fold_in(jax.random.fold_in(keys[7], part), 71), part),
    }


def owner_columns(values, slot_ids, slot_live, block_count):
    tile_kind = slot_ids // block_count
    tile_set = jnp.where((tile_kind == 2)[:, None, None], jnp.swapaxes(values, 1, 2), values)
    onehot = ((slot_ids[:, None] == jnp.arange(3 * block_count, dtype=jnp.int32)[None, :]) & slot_live[:, None]).astype(jnp.float32)
    dense_cols = jnp.einsum("sm,skn->mkn", onehot, tile_set.astype(jnp.float32))
    return dense_cols.astype(jnp.bfloat16).reshape(3, block_count * BLK, BLK)


def reference(tokens, cotangent, fwd_values, fwd_ids, fwd_count, bwd_ids, bwd_count):
    block_count = D // BLK
    token_total = tokens.shape[0]
    tok_blocks_all = tokens.reshape(token_total, block_count, BLK)
    dy_blocks_all = cotangent.reshape(token_total, block_count, BLK)

    def per_owner(dx_sum, owner):
        slot_live = jnp.arange(FCAP, dtype=jnp.int32) < fwd_count[owner]
        dense_cols = owner_columns(fwd_values[owner], fwd_ids[owner], slot_live, block_count)
        gate_pre = jnp.dot(tokens, dense_cols[0], preferred_element_type=jnp.float32)
        up_val = jnp.dot(tokens, dense_cols[1], preferred_element_type=jnp.float32)
        dhidden = jnp.dot(cotangent, dense_cols[2], preferred_element_type=jnp.float32)
        sigmoid_gate = jax.nn.sigmoid(gate_pre)
        activated = gate_pre * sigmoid_gate
        hidden = (activated * up_val).astype(jnp.bfloat16)
        dgate = (dhidden * up_val * sigmoid_gate * (1.0 + gate_pre * (1.0 - sigmoid_gate))).astype(jnp.bfloat16)
        up_grad = (dhidden * activated).astype(jnp.bfloat16)
        dx_term = jnp.dot(dgate, dense_cols[0].T, preferred_element_type=jnp.float32) + jnp.dot(up_grad, dense_cols[1].T, preferred_element_type=jnp.float32)

        back_ids = bwd_ids[owner]
        back_live = jnp.arange(BCAP, dtype=jnp.int32) < bwd_count[owner]
        back_kind = back_ids // block_count
        back_block = back_ids % block_count
        tok_sel = jnp.take(tok_blocks_all, back_block, axis=1)
        dy_sel = jnp.take(dy_blocks_all, back_block, axis=1)
        left_side = jnp.where((back_kind == 2)[None, :, None], hidden[:, None, :], tok_sel)
        right_side = jnp.where((back_kind == 0)[None, :, None], dgate[:, None, :],
                               jnp.where((back_kind == 1)[None, :, None], up_grad[:, None, :], dy_sel))
        left_half = left_side.reshape(N_DP, TOK_DP, BCAP, BLK).astype(jnp.float32)
        right_half = right_side.reshape(N_DP, TOK_DP, BCAP, BLK).astype(jnp.float32)
        half_part = jnp.einsum("ptbk,ptbn->pbkn", left_half, right_half)
        half_part = lax.optimization_barrier(half_part.astype(jnp.bfloat16)).astype(jnp.float32)
        tile_grad = jnp.sum(half_part, axis=0)
        tile_grad = jnp.where(back_live[:, None, None], tile_grad, jnp.float32(0.0)).astype(jnp.bfloat16)
        return dx_sum + dx_term, tile_grad

    dx_total, tile_grads = lax.scan(per_owner, jnp.zeros((token_total, D), jnp.float32), jnp.arange(N_TENSOR, dtype=jnp.int32))
    return dx_total.astype(jnp.bfloat16), tile_grads
```

```python
import functools

import jax
import jax.numpy as jnp
from jax import lax
from jax.experimental import pallas as pl
from jax.experimental.pallas import tpu as pltpu
from jax.sharding import PartitionSpec as P

BF = jnp.bfloat16
F32 = jnp.float32
MIB = 1024 * 1024


def place_tiles(tile_set, slot_ids, slot_live, block_count):
    tile_edge = tile_set.shape[-1]
    onehot = (
        (slot_ids[:, None] == jnp.arange(3 * block_count, dtype=jnp.int32)[None, :])
        & slot_live[:, None]
    ).astype(jnp.bfloat16)
    dense_cols = jnp.einsum("sm,skn->mkn", onehot, tile_set, preferred_element_type=jnp.float32)
    return dense_cols.astype(jnp.bfloat16).reshape(3, block_count * tile_edge, tile_edge)


def gather_plan(tokens, cotangent, fwd_values, fwd_ids, fwd_count, bwd_ids, bwd_count):
    values = fwd_values[0]
    slot_ids = fwd_ids[0]
    slot_count = slot_ids.shape[0]
    tile_edge = values.shape[-1]
    whole_x, whole_dy = (
        lax.all_gather(tokens, "tensor", axis=1, tiled=True),
        lax.all_gather(cotangent, "tensor", axis=1, tiled=True),
    )
    row_count, feature_width = whole_x.shape
    block_count = feature_width // tile_edge
    slot_live = jnp.arange(slot_count, dtype=jnp.int32) < fwd_count[0]
    tile_kind = slot_ids // block_count
    tile_set = jnp.where((tile_kind == 2)[:, None, None], jnp.swapaxes(values, 1, 2), values)
    x_blocks_all = whole_x.reshape(row_count, block_count, tile_edge)
    dy_blocks_all = whole_dy.reshape(row_count, block_count, tile_edge)
    dense_cols = place_tiles(tile_set, slot_ids, slot_live, block_count)
    gate_pre = jnp.dot(whole_x, dense_cols[0], preferred_element_type=jnp.float32)
    up_val = jnp.dot(whole_x, dense_cols[1], preferred_element_type=jnp.float32)
    dhidden = jnp.dot(whole_dy, dense_cols[2], preferred_element_type=jnp.float32)
    hidden, dgate, up_grad = activations(gate_pre, up_val, dhidden)
    contract = (((1,), (1,)), ((), ()))
    dx_term = lax.dot_general(dgate, dense_cols[0], contract, preferred_element_type=jnp.float32)
    dx_term = dx_term + lax.dot_general(
        up_grad, dense_cols[1], contract, preferred_element_type=jnp.float32
    )
    input_grad = lax.psum_scatter(dx_term, "tensor", scatter_dimension=1, tiled=True).astype(
        jnp.bfloat16
    )
    back_ids = bwd_ids[0]
    back_count = back_ids.shape[0]
    back_live = jnp.arange(back_count, dtype=jnp.int32) < bwd_count[0]
    back_kind = back_ids // block_count
    back_block = back_ids % block_count
    tok_sel = jnp.take(x_blocks_all, back_block, axis=1)
    dy_sel = jnp.take(dy_blocks_all, back_block, axis=1)
    left_side = jnp.where((back_kind == 2)[None, :, None], hidden[:, None, :], tok_sel)
    right_side = jnp.where(
        (back_kind == 0)[None, :, None],
        dgate[:, None, :],
        jnp.where((back_kind == 1)[None, :, None], up_grad[:, None, :], dy_sel),
    )
    local_grad = jnp.einsum(
        "tbk,tbn->bkn", left_side, right_side, preferred_element_type=jnp.float32
    )
    local_grad = jnp.where(back_live[:, None, None], local_grad, jnp.float32(0.0))
    summed_grad = lax.psum(local_grad.astype(jnp.bfloat16), "dp")
    return (input_grad, summed_grad[None])


def activations(gate, up, dhidden):
    sig = jax.nn.sigmoid(gate)
    act = gate * sig
    hidden = (act * up).astype(BF)
    dgate = (dhidden * up * sig * (1.0 + gate * (1.0 - sig))).astype(BF)
    dup = (dhidden * act).astype(BF)
    return hidden, dgate, dup


def place_kernel(ids_ref, cnt_ref, where_ref, val_ref, gu_ref, d_ref, *, blocks, edge):
    gu_ref[...] = jnp.zeros_like(gu_ref)
    d_ref[...] = jnp.zeros_like(d_ref)

    def step(s, carry):
        e = ids_ref[s]
        kind = e // blocks
        row = pl.multiple_of(where_ref[e % blocks] * edge, edge)
        tile = val_ref[s]

        @pl.when(kind == 0)
        def _():
            gu_ref[pl.ds(row, edge), 0:edge] = tile

        @pl.when(kind == 1)
        def _():
            gu_ref[pl.ds(row, edge), edge : 2 * edge] = tile

        @pl.when(kind == 2)
        def _():
            d_ref[pl.ds(row, edge), :] = tile.T

        return carry

    lax.fori_loop(0, cnt_ref[0], step, 0)


def place(ids, count, where, values, blocks):
    edge = values.shape[-1]
    width = blocks * edge
    return pl.pallas_call(
        functools.partial(place_kernel, blocks=blocks, edge=edge),
        grid_spec=pltpu.PrefetchScalarGridSpec(
            num_scalar_prefetch=3,
            grid=(1,),
            in_specs=[pl.BlockSpec(values.shape, lambda *_: (0, 0, 0))],
            out_specs=[
                pl.BlockSpec((width, 2 * edge), lambda *_: (0, 0)),
                pl.BlockSpec((width, edge), lambda *_: (0, 0)),
            ],
        ),
        out_shape=[
            jax.ShapeDtypeStruct((width, 2 * edge), BF),
            jax.ShapeDtypeStruct((width, edge), BF),
        ],
        compiler_params=pltpu.CompilerParams(vmem_limit_bytes=24 * MIB),
        cost_estimate=pl.CostEstimate(flops=0, bytes_accessed=8 * MIB, transcendentals=0),
        name="place_weights",
    )(ids, count, where, values)


def grads_kernel(slot_ref, shard_ref, *refs, half, blocks, per, edge, rows):
    mine = refs[: half + 1]
    sib = (None,) + refs[half + 1 : 2 * half] + (None,)
    dgu_m, dgu_s, hid_m, hid_s, out_ref = refs[2 * half :]
    out_ref[...] = jnp.zeros_like(out_ref)
    hm_t = hid_m[...].T
    hs_t = hid_s[...].T

    for d in range(half + 1):
        base = shard_ref[d] * per

        def step(i, carry, d=d, base=base):
            lane = pl.ds(pl.multiple_of(i * edge, edge), edge)
            slots = [slot_ref[k * blocks + base + i] for k in range(3)]

            @pl.when((slots[0] >= 0) | (slots[1] >= 0))
            def _():
                g = jnp.dot(mine[d][0:rows, lane].T, dgu_m[...], preferred_element_type=F32)
                g = g.astype(BF)
                if sib[d] is not None:
                    g2 = jnp.dot(sib[d][0:rows, lane].T, dgu_s[...], preferred_element_type=F32)
                    g = (g.astype(F32) + g2.astype(BF).astype(F32)).astype(BF)

                @pl.when(slots[0] >= 0)
                def _():
                    out_ref[slots[0]] = g[:, 0:edge]

                @pl.when(slots[1] >= 0)
                def _():
                    out_ref[slots[1]] = g[:, edge : 2 * edge]

            @pl.when(slots[2] >= 0)
            def _():
                g = jnp.dot(hm_t, mine[d][rows : 2 * rows, lane], preferred_element_type=F32)
                g = g.astype(BF)
                if sib[d] is not None:
                    g2 = jnp.dot(hs_t, sib[d][rows : 2 * rows, lane], preferred_element_type=F32)
                    g = (g.astype(F32) + g2.astype(BF).astype(F32)).astype(BF)
                out_ref[slots[2]] = g

            return carry

        lax.fori_loop(0, per, step, 0)


def tile_grads(slot_of, shard_of, mine, sib, dgu_m, dgu_s, hid_m, hid_s, slots, blocks):
    rows, edge = hid_m.shape
    half = len(mine) - 1
    arrays = [*mine, *sib, dgu_m, dgu_s, hid_m, hid_s]
    return pl.pallas_call(
        functools.partial(
            grads_kernel,
            half=half,
            blocks=blocks,
            per=mine[0].shape[1] // edge,
            edge=edge,
            rows=rows,
        ),
        grid_spec=pltpu.PrefetchScalarGridSpec(
            num_scalar_prefetch=2,
            grid=(1,),
            in_specs=[pl.BlockSpec(a.shape, lambda *_: (0, 0)) for a in arrays],
            out_specs=pl.BlockSpec((slots, edge, edge), lambda *_: (0, 0, 0)),
        ),
        out_shape=jax.ShapeDtypeStruct((slots, edge, edge), BF),
        compiler_params=pltpu.CompilerParams(vmem_limit_bytes=24 * MIB),
        cost_estimate=pl.CostEstimate(
            flops=800_000_000, bytes_accessed=8 * MIB, transcendentals=0
        ),
        name="tile_gradients",
    )(slot_of, shard_of, *arrays)


def pick(table, index):
    n = table.shape[0]
    hit = index[:, None] == jnp.arange(n, dtype=jnp.int32)[None, :]
    return jnp.sum(jnp.where(hit, table[None, :], 0), axis=1, dtype=jnp.int32)


def ring_plan(tokens, cotangent, fwd_values, fwd_ids, fwd_count, bwd_ids, bwd_count, *, n):
    half = n // 2
    ring = [2 * i for i in range(half)] + [2 * i + 1 for i in reversed(range(half))]
    pos = [ring.index(t) for t in range(n)]
    perm = []
    for i in range(n):
        perm.append((ring[i] * 2, ring[(i + 1) % n] * 2))
        perm.append((ring[i] * 2 + 1, ring[(i - 1) % n] * 2 + 1))
    hop = lambda v: lax.ppermute(v, ("tensor", "dp"), perm)
    swap = lambda v: lax.ppermute(v, "dp", [(0, 1), (1, 0)])

    values = fwd_values[0]
    edge = values.shape[-1]
    rows, width = tokens.shape
    per = width // edge
    blocks = n * per
    slots = bwd_ids.shape[1]

    core = lax.axis_index("dp")
    sign = 1 - 2 * core
    here = pick(jnp.array(pos, jnp.int32), lax.axis_index("tensor")[None])[0]
    steps = jnp.arange(n, dtype=jnp.int32)
    shard_of = pick(jnp.array(ring, jnp.int32), (here - sign * steps) % n)
    dist_of = ((here - jnp.array(pos, jnp.int32)) * sign) % n
    where = (dist_of[:, None] * per + jnp.arange(per, dtype=jnp.int32)[None, :]).reshape(blocks)
    slot_iota = jnp.arange(slots, dtype=jnp.int32)
    hit = (bwd_ids[0][None, :] == jnp.arange(3 * blocks, dtype=jnp.int32)[:, None]) & (
        slot_iota < bwd_count[0]
    )[None, :]
    slot_of = jnp.max(jnp.where(hit, slot_iota[None, :], -1), axis=1)

    own = jnp.concatenate([tokens, cotangent], axis=0)
    mine = [own]
    sib = [swap(own)]
    for k in range(1, half + 1):
        mine.append(hop(mine[-1]))
        if k < half:
            sib.append(hop(sib[-1]))

    w_gu, w_d = place(fwd_ids[0], fwd_count, where, values, blocks)
    gu_at = lambda d: w_gu[d * width : (d + 1) * width]
    d_at = lambda d: w_d[d * width : (d + 1) * width]
    dot = functools.partial(jnp.dot, preferred_element_type=F32)

    gu_m = dot(mine[0][:rows], gu_at(0))
    dh_m = dot(mine[0][rows:], d_at(0))
    gu_s = dh_s = None
    for d in range(1, half + 1):
        gu_m = gu_m + dot(mine[d][:rows], gu_at(d))
        dh_m = dh_m + dot(mine[d][rows:], d_at(d))
        if d < half:
            part = dot(sib[d][:rows], gu_at(d))
            gu_s = part if gu_s is None else gu_s + part
            part = dot(sib[d][rows:], d_at(d))
            dh_s = part if dh_s is None else dh_s + part
    gu_tm, gu_ts = gu_m + swap(gu_s), gu_s + swap(gu_m)
    dh_tm, dh_ts = dh_m + swap(dh_s), dh_s + swap(dh_m)

    hid_m, dg_m, du_m = activations(gu_tm[:, :edge], gu_tm[:, edge:], dh_tm)
    hid_s, dg_s, du_s = activations(gu_ts[:, :edge], gu_ts[:, edge:], dh_ts)
    dgu_m = jnp.concatenate([dg_m, du_m], axis=1)
    dgu_s = jnp.concatenate([dg_s, du_s], axis=1)

    term = lambda dgu, d: lax.dot_general(
        dgu, gu_at(d), (((1,), (1,)), ((), ())), preferred_element_type=F32
    )
    run_m = hop(term(dgu_m, half).astype(BF))
    run_s = None
    for d in range(half + 1, n):
        part = term(dgu_s, d)
        run_s = hop((part if run_s is None else part + run_s.astype(F32)).astype(BF))
        run_m = hop((term(dgu_m, d) + run_m.astype(F32)).astype(BF))
    dx = term(dgu_m, 0) + run_m.astype(F32) + swap(run_s).astype(F32)

    grads = tile_grads(
        slot_of, shard_of, mine, sib[1:], dgu_m, dgu_s, hid_m, hid_s, slots, blocks
    )
    grads = grads + swap(grads)
    return dx.astype(BF), grads[None]


def on_device(tokens, cotangent, fwd_values, *rest, n, cores):
    width, edge = tokens.shape[1], fwd_values.shape[-1]
    if cores == 2 and n % 2 == 0 and 4 <= n <= 16 and width % edge == 0:
        return ring_plan(tokens, cotangent, fwd_values, *rest, n=n)
    return gather_plan(tokens, cotangent, fwd_values, *rest)


def solution(mesh):
    return jax.shard_map(
        functools.partial(on_device, n=mesh.shape["tensor"], cores=mesh.shape["dp"]),
        mesh=mesh,
        in_specs=(
            P(("groups", "dp"), "tensor"),
            P(("groups", "dp"), "tensor"),
            P(("groups", "tensor"), None, None, None),
            P(("groups", "tensor"), None),
            P(("groups", "tensor")),
            P(("groups", "tensor"), None),
            P(("groups", "tensor")),
        ),
        out_specs=(P(("groups", "dp"), "tensor"), P(("groups", "tensor"), None, None, None)),
        check_vma=False,
    )
```

```python
import functools

import jax
import jax.numpy as jnp
from jax import lax
from jax.experimental import pallas as pl
from jax.experimental.pallas import tpu as pltpu
from jax.sharding import PartitionSpec as P

BF = jnp.bfloat16
F32 = jnp.float32
MIB = 1024 * 1024


def place_tiles(tile_set, slot_ids, slot_live, block_count):
    tile_edge = tile_set.shape[-1]
    onehot = (
        (slot_ids[:, None] == jnp.arange(3 * block_count, dtype=jnp.int32)[None, :])
        & slot_live[:, None]
    ).astype(jnp.bfloat16)
    dense_cols = jnp.einsum("sm,skn->mkn", onehot, tile_set, preferred_element_type=jnp.float32)
    return dense_cols.astype(jnp.bfloat16).reshape(3, block_count * tile_edge, tile_edge)


def gather_plan(tokens, cotangent, fwd_values, fwd_ids, fwd_count, bwd_ids, bwd_count):
    values = fwd_values[0]
    slot_ids = fwd_ids[0]
    slot_count = slot_ids.shape[0]
    tile_edge = values.shape[-1]
    whole_x, whole_dy = (
        lax.all_gather(tokens, "tensor", axis=1, tiled=True),
        lax.all_gather(cotangent, "tensor", axis=1, tiled=True),
    )
    row_count, feature_width = whole_x.shape
    block_count = feature_width // tile_edge
    slot_live = jnp.arange(slot_count, dtype=jnp.int32) < fwd_count[0]
    tile_kind = slot_ids // block_count
    tile_set = jnp.where((tile_kind == 2)[:, None, None], jnp.swapaxes(values, 1, 2), values)
    x_blocks_all = whole_x.reshape(row_count, block_count, tile_edge)
    dy_blocks_all = whole_dy.reshape(row_count, block_count, tile_edge)
    dense_cols = place_tiles(tile_set, slot_ids, slot_live, block_count)
    gate_pre = jnp.dot(whole_x, dense_cols[0], preferred_element_type=jnp.float32)
    up_val = jnp.dot(whole_x, dense_cols[1], preferred_element_type=jnp.float32)
    dhidden = jnp.dot(whole_dy, dense_cols[2], preferred_element_type=jnp.float32)
    hidden, dgate, up_grad = activations(gate_pre, up_val, dhidden)
    contract = (((1,), (1,)), ((), ()))
    dx_term = lax.dot_general(dgate, dense_cols[0], contract, preferred_element_type=jnp.float32)
    dx_term = dx_term + lax.dot_general(
        up_grad, dense_cols[1], contract, preferred_element_type=jnp.float32
    )
    input_grad = lax.psum_scatter(dx_term, "tensor", scatter_dimension=1, tiled=True).astype(
        jnp.bfloat16
    )
    back_ids = bwd_ids[0]
    back_count = back_ids.shape[0]
    back_live = jnp.arange(back_count, dtype=jnp.int32) < bwd_count[0]
    back_kind = back_ids // block_count
    back_block = back_ids % block_count
    tok_sel = jnp.take(x_blocks_all, back_block, axis=1)
    dy_sel = jnp.take(dy_blocks_all, back_block, axis=1)
    left_side = jnp.where((back_kind == 2)[None, :, None], hidden[:, None, :], tok_sel)
    right_side = jnp.where(
        (back_kind == 0)[None, :, None],
        dgate[:, None, :],
        jnp.where((back_kind == 1)[None, :, None], up_grad[:, None, :], dy_sel),
    )
    local_grad = jnp.einsum(
        "tbk,tbn->bkn", left_side, right_side, preferred_element_type=jnp.float32
    )
    local_grad = jnp.where(back_live[:, None, None], local_grad, jnp.float32(0.0))
    summed_grad = lax.psum(local_grad.astype(jnp.bfloat16), "dp")
    return (input_grad, summed_grad[None])


def activations(gate, up, dhidden):
    sig = jax.nn.sigmoid(gate)
    act = gate * sig
    hidden = (act * up).astype(BF)
    dgate = (dhidden * up * sig * (1.0 + gate * (1.0 - sig))).astype(BF)
    dup = (dhidden * act).astype(BF)
    return hidden, dgate, dup


def place_kernel(ids_ref, cnt_ref, where_ref, val_ref, _, gu_ref, d_ref, *, blocks, edge):
    gu_ref[...] = jnp.zeros_like(gu_ref)
    d_ref[...] = jnp.zeros_like(d_ref)

    def step(s, carry):
        e = ids_ref[s]
        kind = e // blocks
        row = pl.multiple_of(where_ref[e % blocks] * edge, edge)
        tile = val_ref[s]

        @pl.when(kind == 0)
        def _():
            gu_ref[pl.ds(row, edge), 0:edge] = tile

        @pl.when(kind == 1)
        def _():
            gu_ref[pl.ds(row, edge), edge : 2 * edge] = tile

        @pl.when(kind == 2)
        def _():
            d_ref[pl.ds(row, edge), :] = tile.T

        return carry

    lax.fori_loop(0, cnt_ref[0], step, 0)


def place(ids, count, where, values, after, blocks):
    edge = values.shape[-1]
    width = blocks * edge
    return pl.pallas_call(
        functools.partial(place_kernel, blocks=blocks, edge=edge),
        grid_spec=pltpu.PrefetchScalarGridSpec(
            num_scalar_prefetch=3,
            grid=(1,),
            in_specs=[
                pl.BlockSpec(values.shape, lambda *_: (0, 0, 0)),
                pl.BlockSpec(memory_space=pl.ANY),
            ],
            out_specs=[
                pl.BlockSpec((width, 2 * edge), lambda *_: (0, 0)),
                pl.BlockSpec((width, edge), lambda *_: (0, 0)),
            ],
        ),
        out_shape=[
            jax.ShapeDtypeStruct((width, 2 * edge), BF),
            jax.ShapeDtypeStruct((width, edge), BF),
        ],
        compiler_params=pltpu.CompilerParams(vmem_limit_bytes=24 * MIB),
        cost_estimate=pl.CostEstimate(flops=0, bytes_accessed=8 * MIB, transcendentals=0),
        name="place_weights",
    )(ids, count, where, values, after)


def grads_kernel(src_ref, *refs, half, edge):
    refs = list(refs)
    take = lambda k: [refs.pop(0) for _ in range(k)]
    x_m, y_m = take(half + 1), take(half + 1)
    x_s, y_s = take(half - 1), take(half - 1)
    dgu_m, dgu_s, hid_m, hid_s, _, out_ref, all_ref = take(7)
    per = x_m[0].shape[1] // edge
    left = (((0,), (0,)), ((), ()))
    dot = lambda a, b: lax.dot_general(a, b, left, preferred_element_type=F32).astype(BF)
    both = lambda a, b: (a.astype(F32) + b.astype(F32)).astype(BF)
    hm, hs = hid_m[...], hid_s[...]

    for d in range(half + 1):
        base = d * per * 3
        pair = 0 < d < half
        for i in range(per):
            lane = slice(i * edge, (i + 1) * edge)
            g = dot(x_m[d][:, lane], dgu_m[...])
            h = dot(hm, y_m[d][:, lane])
            if pair:
                g = both(g, dot(x_s[d - 1][:, lane], dgu_s[...]))
                h = both(h, dot(hs, y_s[d - 1][:, lane]))
            all_ref[base + 3 * i] = g[:, :edge]
            all_ref[base + 3 * i + 1] = g[:, edge:]
            all_ref[base + 3 * i + 2] = h
    all_ref[(half + 1) * per * 3] = jnp.zeros((edge, edge), BF)

    def step(s, carry):
        out_ref[s] = all_ref[src_ref[s]]
        return carry

    lax.fori_loop(0, out_ref.shape[0], step, 0, unroll=4)


def tile_grads(src, x_m, y_m, x_s, y_s, dgu_m, dgu_s, hid_m, hid_s, after):
    edge = hid_m.shape[1]
    half = len(x_m) - 1
    slots = src.shape[0]
    tiles = (half + 1) * (x_m[0].shape[1] // edge) * 3 + 1
    arrays = [*x_m, *y_m, *x_s, *y_s, dgu_m, dgu_s, hid_m, hid_s]
    return pl.pallas_call(
        functools.partial(grads_kernel, half=half, edge=edge),
        grid_spec=pltpu.PrefetchScalarGridSpec(
            num_scalar_prefetch=1,
            grid=(1,),
            in_specs=[pl.BlockSpec(a.shape, lambda *_: (0, 0)) for a in arrays]
            + [pl.BlockSpec(memory_space=pl.ANY)],
            out_specs=pl.BlockSpec((slots, edge, edge), lambda *_: (0, 0, 0)),
            scratch_shapes=[pltpu.VMEM((tiles, edge, edge), BF)],
        ),
        out_shape=jax.ShapeDtypeStruct((slots, edge, edge), BF),
        compiler_params=pltpu.CompilerParams(vmem_limit_bytes=28 * MIB),
        cost_estimate=pl.CostEstimate(
            flops=800_000_000, bytes_accessed=8 * MIB, transcendentals=0
        ),
        name="tile_gradients",
    )(src, *arrays, after)


def pick(table, index):
    n = table.shape[0]
    hit = index[:, None] == jnp.arange(n, dtype=jnp.int32)[None, :]
    return jnp.sum(jnp.where(hit, table[None, :], 0), axis=1, dtype=jnp.int32)


def ring_plan(tokens, cotangent, fwd_values, fwd_ids, fwd_count, bwd_ids, bwd_count, *, n):
    half = n // 2
    ring = [2 * i for i in range(half)] + [2 * i + 1 for i in reversed(range(half))]
    pos = [ring.index(t) for t in range(n)]
    perm = []
    for i in range(n):
        perm.append((ring[i] * 2, ring[(i + 1) % n] * 2))
        perm.append((ring[i] * 2 + 1, ring[(i - 1) % n] * 2 + 1))
    hop = lambda v: lax.ppermute(v, ("tensor", "dp"), perm)
    swap = lambda v: lax.ppermute(v, "dp", [(0, 1), (1, 0)])

    values = fwd_values[0]
    edge = values.shape[-1]
    width = tokens.shape[1]
    per = width // edge
    blocks = n * per
    slots = bwd_ids.shape[1]

    x_m, y_m = [tokens], [cotangent]
    x_s, y_s = [swap(tokens)], [swap(cotangent)]
    for k in range(1, half + 1):
        x_m.append(hop(x_m[-1]))
        y_m.append(hop(y_m[-1]))
        if k < half:
            x_s.append(hop(x_s[-1]))
            y_s.append(hop(y_s[-1]))

    core = lax.axis_index("dp")
    sign = 1 - 2 * core
    here = pick(jnp.array(pos, jnp.int32), lax.axis_index("tensor")[None])[0]
    dist_of = ((here - jnp.array(pos, jnp.int32)) * sign) % n
    where = (dist_of[:, None] * per + jnp.arange(per, dtype=jnp.int32)[None, :]).reshape(blocks)
    back = bwd_ids[0]
    spot = pick(where, back % blocks)
    held = (spot < (half + 1) * per) & (jnp.arange(slots, dtype=jnp.int32) < bwd_count[0])
    src = jnp.where(held, spot * 3 + back // blocks, (half + 1) * per * 3)

    w_gu, w_d = place(fwd_ids[0], fwd_count, where, values, y_s[0], blocks)
    gu_at = lambda d: w_gu[d * width : (d + 1) * width]
    d_at = lambda d: w_d[d * width : (d + 1) * width]
    dot = functools.partial(jnp.dot, preferred_element_type=F32)

    gu_m, dh_m = dot(x_m[0], gu_at(0)), dot(y_m[0], d_at(0))
    gu_s, dh_s = dot(x_s[1], gu_at(1)), dot(y_s[1], d_at(1))
    for d in range(1, half + 1):
        gu_m = gu_m + dot(x_m[d], gu_at(d))
        dh_m = dh_m + dot(y_m[d], d_at(d))
        if 1 < d < half:
            gu_s = gu_s + dot(x_s[d], gu_at(d))
            dh_s = dh_s + dot(y_s[d], d_at(d))
    gu_tm, dh_tm = gu_m + swap(gu_s), dh_m + swap(dh_s)
    gu_ts, dh_ts = gu_s + swap(gu_m), dh_s + swap(dh_m)

    hid_m, dg_m, du_m = activations(gu_tm[:, :edge], gu_tm[:, edge:], dh_tm)
    hid_s, dg_s, du_s = activations(gu_ts[:, :edge], gu_ts[:, edge:], dh_ts)
    dgu_m = jnp.concatenate([dg_m, du_m], axis=1)
    dgu_s = jnp.concatenate([dg_s, du_s], axis=1)

    part = width // 2

    def term(dgu, d, p):
        rows = w_gu[d * width + p * part : d * width + (p + 1) * part]
        return lax.dot_general(dgu, rows, (((1,), (1,)), ((), ())), preferred_element_type=F32)

    run_m = [hop(term(dgu_m, half, p).astype(BF)) for p in range(2)]
    run_s = [None, None]
    first = None
    for d in range(half + 1, n):
        for p in range(2):
            out = term(dgu_s, d, p)
            if run_s[p] is not None:
                out = out + run_s[p].astype(F32)
            run_s[p] = hop(out.astype(BF))
        if first is None:
            first = run_s[0]
        for p in range(2):
            run_m[p] = hop((term(dgu_m, d, p) + run_m[p].astype(F32)).astype(BF))
    dx = [
        (term(dgu_m, 0, p) + run_m[p].astype(F32) + swap(run_s[p]).astype(F32)).astype(BF)
        for p in range(2)
    ]

    grads = tile_grads(
        src, x_m, y_m, x_s[1:half], y_s[1:half], dgu_m, dgu_s, hid_m, hid_s, first
    )
    grads = grads + swap(grads)
    return jnp.concatenate(dx, axis=1), grads[None]


def on_device(tokens, cotangent, fwd_values, *rest, n, cores):
    width, edge = tokens.shape[1], fwd_values.shape[-1]
    if cores == 2 and n % 2 == 0 and 4 <= n <= 16 and width % edge == 0:
        return ring_plan(tokens, cotangent, fwd_values, *rest, n=n)
    return gather_plan(tokens, cotangent, fwd_values, *rest)


def solution(mesh):
    return jax.shard_map(
        functools.partial(on_device, n=mesh.shape["tensor"], cores=mesh.shape["dp"]),
        mesh=mesh,
        in_specs=(
            P(("groups", "dp"), "tensor"),
            P(("groups", "dp"), "tensor"),
            P(("groups", "tensor"), None, None, None),
            P(("groups", "tensor"), None),
            P(("groups", "tensor")),
            P(("groups", "tensor"), None),
            P(("groups", "tensor")),
        ),
        out_specs=(P(("groups", "dp"), "tensor"), P(("groups", "tensor"), None, None, None)),
        check_vma=False,
    )
```

```python
import functools

import jax
import jax.numpy as jnp
from jax import lax
from jax.experimental import pallas as pl
from jax.experimental.pallas import tpu as pltpu
from jax.sharding import PartitionSpec as P

BF = jnp.bfloat16
F32 = jnp.float32
MIB = 1024 * 1024
LITTLE = pl.CostEstimate(flops=1, bytes_accessed=1, transcendentals=0)


def place_tiles(tile_set, slot_ids, slot_live, block_count):
    tile_edge = tile_set.shape[-1]
    onehot = (
        (slot_ids[:, None] == jnp.arange(3 * block_count, dtype=jnp.int32)[None, :])
        & slot_live[:, None]
    ).astype(jnp.bfloat16)
    dense_cols = jnp.einsum("sm,skn->mkn", onehot, tile_set, preferred_element_type=jnp.float32)
    return dense_cols.astype(jnp.bfloat16).reshape(3, block_count * tile_edge, tile_edge)


def gather_plan(tokens, cotangent, fwd_values, fwd_ids, fwd_count, bwd_ids, bwd_count):
    values = fwd_values[0]
    slot_ids = fwd_ids[0]
    slot_count = slot_ids.shape[0]
    tile_edge = values.shape[-1]
    whole_x, whole_dy = (
        lax.all_gather(tokens, "tensor", axis=1, tiled=True),
        lax.all_gather(cotangent, "tensor", axis=1, tiled=True),
    )
    row_count, feature_width = whole_x.shape
    block_count = feature_width // tile_edge
    slot_live = jnp.arange(slot_count, dtype=jnp.int32) < fwd_count[0]
    tile_kind = slot_ids // block_count
    tile_set = jnp.where((tile_kind == 2)[:, None, None], jnp.swapaxes(values, 1, 2), values)
    x_blocks_all = whole_x.reshape(row_count, block_count, tile_edge)
    dy_blocks_all = whole_dy.reshape(row_count, block_count, tile_edge)
    dense_cols = place_tiles(tile_set, slot_ids, slot_live, block_count)
    gate_pre = jnp.dot(whole_x, dense_cols[0], preferred_element_type=jnp.float32)
    up_val = jnp.dot(whole_x, dense_cols[1], preferred_element_type=jnp.float32)
    dhidden = jnp.dot(whole_dy, dense_cols[2], preferred_element_type=jnp.float32)
    hidden, dgate, up_grad = activations(gate_pre, up_val, dhidden)
    contract = (((1,), (1,)), ((), ()))
    dx_term = lax.dot_general(dgate, dense_cols[0], contract, preferred_element_type=jnp.float32)
    dx_term = dx_term + lax.dot_general(
        up_grad, dense_cols[1], contract, preferred_element_type=jnp.float32
    )
    input_grad = lax.psum_scatter(dx_term, "tensor", scatter_dimension=1, tiled=True).astype(
        jnp.bfloat16
    )
    back_ids = bwd_ids[0]
    back_count = back_ids.shape[0]
    back_live = jnp.arange(back_count, dtype=jnp.int32) < bwd_count[0]
    back_kind = back_ids // block_count
    back_block = back_ids % block_count
    tok_sel = jnp.take(x_blocks_all, back_block, axis=1)
    dy_sel = jnp.take(dy_blocks_all, back_block, axis=1)
    left_side = jnp.where((back_kind == 2)[None, :, None], hidden[:, None, :], tok_sel)
    right_side = jnp.where(
        (back_kind == 0)[None, :, None],
        dgate[:, None, :],
        jnp.where((back_kind == 1)[None, :, None], up_grad[:, None, :], dy_sel),
    )
    local_grad = jnp.einsum(
        "tbk,tbn->bkn", left_side, right_side, preferred_element_type=jnp.float32
    )
    local_grad = jnp.where(back_live[:, None, None], local_grad, jnp.float32(0.0))
    summed_grad = lax.psum(local_grad.astype(jnp.bfloat16), "dp")
    return (input_grad, summed_grad[None])


def activations(gate, up, dhidden):
    sig = jax.nn.sigmoid(gate)
    act = gate * sig
    hidden = (act * up).astype(BF)
    dgate = (dhidden * up * sig * (1.0 + gate * (1.0 - sig))).astype(BF)
    dup = (dhidden * act).astype(BF)
    return hidden, dgate, dup


def split(value, size):
    if size & (size - 1) == 0:
        return value >> (size.bit_length() - 1), value & (size - 1)
    return lax.div(value, size), lax.rem(value, size)


def spot_of(block, here_ref, n, per):
    shard, inner = split(block, per)
    up, odd = split(shard, 2)
    at = jnp.where(odd == 1, n - 1 - up, up)
    _, dist = split((here_ref[0] - at) * here_ref[1] + n, n)
    return dist * per + inner


def place_kernel(here_ref, ids_ref, cnt_ref, val_ref, gu_ref, d_ref, *, n, blocks, edge):
    gu_ref[...] = jnp.zeros_like(gu_ref)
    d_ref[...] = jnp.zeros_like(d_ref)

    def step(s, carry):
        e = ids_ref[s]
        kind, block = split(e, blocks)
        row = pl.multiple_of(spot_of(block, here_ref, n, blocks // n) * edge, edge)
        tile = val_ref[s]

        @pl.when(kind == 0)
        def _():
            gu_ref[pl.ds(row, edge), 0:edge] = tile

        @pl.when(kind == 1)
        def _():
            gu_ref[pl.ds(row, edge), edge : 2 * edge] = tile

        @pl.when(kind == 2)
        def _():
            d_ref[pl.ds(row, edge), :] = tile.T

        return carry

    lax.fori_loop(0, cnt_ref[0], step, 0)


def place(here, ids, count, values, n, blocks):
    edge = values.shape[-1]
    width = blocks * edge
    return pl.pallas_call(
        functools.partial(place_kernel, n=n, blocks=blocks, edge=edge),
        grid_spec=pltpu.PrefetchScalarGridSpec(
            num_scalar_prefetch=3,
            grid=(1,),
            in_specs=[pl.BlockSpec(values.shape, lambda *_: (0, 0, 0))],
            out_specs=[
                pl.BlockSpec((width, 2 * edge), lambda *_: (0, 0)),
                pl.BlockSpec((width, edge), lambda *_: (0, 0)),
            ],
        ),
        out_shape=[
            jax.ShapeDtypeStruct((width, 2 * edge), BF),
            jax.ShapeDtypeStruct((width, edge), BF),
        ],
        compiler_params=pltpu.CompilerParams(vmem_limit_bytes=24 * MIB),
        cost_estimate=LITTLE,
        name="place_weights",
    )(here, ids, count, values)


def forward_kernel(*refs, half, width):
    refs = list(refs)
    take = lambda k: [refs.pop(0) for _ in range(k)]
    x_m, y_m, x_s, y_s = take(half), take(half), take(half - 1), take(half - 1)
    w_gu, w_d, gu_m, dh_m, gu_s, dh_s = refs

    def total(parts, w, first):
        out = None
        for d, part in enumerate(parts, first):
            rows = w[d * width : (d + 1) * width, :]
            term = jnp.dot(part[...], rows, preferred_element_type=F32)
            out = term if out is None else out + term
        return out

    gu_m[...] = total(x_m, w_gu, 0)
    dh_m[...] = total(y_m, w_d, 0)
    gu_s[...] = total(x_s, w_gu, 1)
    dh_s[...] = total(y_s, w_d, 1)


def forward(x_m, y_m, x_s, y_s, w_gu, w_d):
    half = len(x_m)
    rows, width = x_m[0].shape
    edge = w_d.shape[1]
    whole = lambda shape: pl.BlockSpec(shape, lambda *_: (0, 0))
    gu, dh = (rows, 2 * edge), (rows, edge)
    arrays = [*x_m, *y_m, *x_s, *y_s, w_gu, w_d]
    return pl.pallas_call(
        functools.partial(forward_kernel, half=half, width=width),
        grid=(1,),
        in_specs=[whole(a.shape) for a in arrays],
        out_specs=[whole(gu), whole(dh), whole(gu), whole(dh)],
        out_shape=[jax.ShapeDtypeStruct(t, F32) for t in (gu, dh, gu, dh)],
        compiler_params=pltpu.CompilerParams(vmem_limit_bytes=28 * MIB),
        cost_estimate=LITTLE,
        name="forward_terms",
    )(*arrays)


def grads_kernel(here_ref, ids_ref, cnt_ref, *refs, half, blocks, edge):
    refs = list(refs)
    take = lambda k: [refs.pop(0) for _ in range(k)]
    x_m, y_m = take(half + 1), take(half + 1)
    x_s, y_s = take(half - 1), take(half - 1)
    dgu_m, dgu_s, hid_m, hid_s = take(4)
    out_ref, all_ref = refs[-2:]
    per = x_m[0].shape[1] // edge
    left = (((0,), (0,)), ((), ()))
    dot = lambda a, b: lax.dot_general(a, b, left, preferred_element_type=F32).astype(BF)
    both = lambda a, b: (a.astype(F32) + b.astype(F32)).astype(BF)
    hm, hs = hid_m[...], hid_s[...]

    for d in range(half + 1):
        base = d * per * 3
        pair = 0 < d < half
        for i in range(per):
            lane = slice(i * edge, (i + 1) * edge)
            g = dot(x_m[d][:, lane], dgu_m[...])
            h = dot(hm, y_m[d][:, lane])
            if pair:
                g = both(g, dot(x_s[d - 1][:, lane], dgu_s[...]))
                h = both(h, dot(hs, y_s[d - 1][:, lane]))
            all_ref[base + 3 * i] = g[:, :edge]
            all_ref[base + 3 * i + 1] = g[:, edge:]
            all_ref[base + 3 * i + 2] = h
    none = (half + 1) * per * 3
    all_ref[none] = jnp.zeros((edge, edge), BF)
    count = cnt_ref[0]

    def step(s, carry):
        e = ids_ref[s]
        kind, block = split(e, blocks)
        spot = spot_of(block, here_ref, 2 * half, per)
        held = (s < count) & (spot < (half + 1) * per)
        out_ref[s] = all_ref[jnp.where(held, spot * 3 + kind, none)]
        return carry

    lax.fori_loop(0, out_ref.shape[0], step, 0, unroll=4)


def tile_grads(here, ids, count, x_m, y_m, x_s, y_s, dgu_m, dgu_s, hid_m, hid_s, blocks):
    edge = hid_m.shape[1]
    half = len(x_m) - 1
    slots = ids.shape[0]
    tiles = (half + 1) * (x_m[0].shape[1] // edge) * 3 + 1
    arrays = [*x_m, *y_m, *x_s, *y_s, dgu_m, dgu_s, hid_m, hid_s]
    return pl.pallas_call(
        functools.partial(grads_kernel, half=half, blocks=blocks, edge=edge),
        grid_spec=pltpu.PrefetchScalarGridSpec(
            num_scalar_prefetch=3,
            grid=(1,),
            in_specs=[pl.BlockSpec(a.shape, lambda *_: (0, 0)) for a in arrays],
            out_specs=pl.BlockSpec((slots, edge, edge), lambda *_: (0, 0, 0)),
            scratch_shapes=[pltpu.VMEM((tiles, edge, edge), BF)],
        ),
        out_shape=jax.ShapeDtypeStruct((slots, edge, edge), BF),
        compiler_params=pltpu.CompilerParams(vmem_limit_bytes=28 * MIB),
        cost_estimate=LITTLE,
        name="tile_gradients",
    )(here, ids, count, *arrays)


def ring_plan(tokens, cotangent, fwd_values, fwd_ids, fwd_count, bwd_ids, bwd_count, *, n):
    half = n // 2
    ring = [2 * i for i in range(half)] + [2 * i + 1 for i in reversed(range(half))]
    perm, cross = [], []
    for i in range(n):
        ahead, behind = ring[(i + 1) % n], ring[(i - 1) % n]
        perm += [(ring[i] * 2, ahead * 2), (ring[i] * 2 + 1, behind * 2 + 1)]
        cross += [(ring[i] * 2 + 1, ahead * 2), (ring[i] * 2, behind * 2 + 1)]
    axes = ("tensor", "dp")
    hop = lambda v: lax.ppermute(v, axes, perm)
    swap = lambda v: lax.ppermute(v, "dp", [(0, 1), (1, 0)])

    values = fwd_values[0]
    edge = values.shape[-1]
    width = tokens.shape[1]
    blocks = n * (width // edge)

    shard = lax.axis_index("tensor")
    here = jnp.stack(
        [
            jnp.where(shard % 2 == 1, n - 1 - shard // 2, shard // 2),
            1 - 2 * lax.axis_index("dp"),
        ]
    ).astype(jnp.int32)
    w_gu, w_d = place(here, fwd_ids[0], fwd_count, values, n, blocks)

    x_m, y_m = [tokens, hop(tokens)], [cotangent, hop(cotangent)]
    x_s, y_s = [lax.ppermute(tokens, axes, cross)], [lax.ppermute(cotangent, axes, cross)]
    x_m[1], w_gu, w_d = lax.optimization_barrier((x_m[1], w_gu, w_d))
    for k in range(2, half + 1):
        x_m.append(hop(x_m[-1]))
        y_m.append(hop(y_m[-1]))
        if k < half:
            x_s.append(hop(x_s[-1]))
            y_s.append(hop(y_s[-1]))

    gu_m, dh_m, gu_s, dh_s = forward(x_m[:half], y_m[:half], x_s, y_s, w_gu, w_d)
    last = slice(half * width, (half + 1) * width)
    gu_m = gu_m + jnp.dot(x_m[half], w_gu[last], preferred_element_type=F32)
    dh_m = dh_m + jnp.dot(y_m[half], w_d[last], preferred_element_type=F32)
    gu_tm, dh_tm = gu_m + swap(gu_s), dh_m + swap(dh_s)
    gu_ts, dh_ts = gu_s + swap(gu_m), dh_s + swap(dh_m)

    hid_m, dg_m, du_m = activations(gu_tm[:, :edge], gu_tm[:, edge:], dh_tm)
    hid_s, dg_s, du_s = activations(gu_ts[:, :edge], gu_ts[:, edge:], dh_ts)
    dgu_m = jnp.concatenate([dg_m, du_m], axis=1)
    dgu_s = jnp.concatenate([dg_s, du_s], axis=1)

    part = width // 2

    def term(dgu, d, p):
        rows = w_gu[d * width + p * part : d * width + (p + 1) * part]
        return lax.dot_general(dgu, rows, (((1,), (1,)), ((), ())), preferred_element_type=F32)

    run_m = [hop(term(dgu_m, half, p).astype(BF)) for p in range(2)]
    run_s = [None, None]
    for d in range(half + 1, n):
        for p in range(2):
            out = term(dgu_s, d, p)
            if run_s[p] is not None:
                out = out + run_s[p].astype(F32)
            run_s[p] = hop(out.astype(BF))
        for p in range(2):
            run_m[p] = hop((term(dgu_m, d, p) + run_m[p].astype(F32)).astype(BF))
    back = [swap(v) for v in run_s]

    grads = tile_grads(
        here, bwd_ids[0], bwd_count, x_m, y_m, x_s, y_s, dgu_m, dgu_s, hid_m, hid_s, blocks
    )
    grads = grads + swap(grads)
    run_m[0], run_m[1], grads = lax.optimization_barrier((run_m[0], run_m[1], grads))
    dx = [
        (term(dgu_m, 0, p) + run_m[p].astype(F32) + back[p].astype(F32)).astype(BF)
        for p in range(2)
    ]
    return jnp.concatenate(dx, axis=1), grads[None]


def on_device(tokens, cotangent, fwd_values, *rest, n, cores):
    width, edge = tokens.shape[1], fwd_values.shape[-1]
    if cores == 2 and n % 2 == 0 and 4 <= n <= 16 and width % edge == 0:
        return ring_plan(tokens, cotangent, fwd_values, *rest, n=n)
    return gather_plan(tokens, cotangent, fwd_values, *rest)


def solution(mesh):
    return jax.shard_map(
        functools.partial(on_device, n=mesh.shape["tensor"], cores=mesh.shape["dp"]),
        mesh=mesh,
        in_specs=(
            P(("groups", "dp"), "tensor"),
            P(("groups", "dp"), "tensor"),
            P(("groups", "tensor"), None, None, None),
            P(("groups", "tensor"), None),
            P(("groups", "tensor")),
            P(("groups", "tensor"), None),
            P(("groups", "tensor")),
        ),
        out_specs=(P(("groups", "dp"), "tensor"), P(("groups", "tensor"), None, None, None)),
        check_vma=False,
    )
```

```python
import functools

import jax
import jax.numpy as jnp
from jax import lax
from jax.experimental import pallas as pl
from jax.experimental.pallas import tpu as pltpu
from jax.sharding import PartitionSpec as P

BF = jnp.bfloat16
F32 = jnp.float32
MIB = 1024 * 1024
VMEM = pl.BlockSpec(memory_space=pltpu.VMEM)
SMEM = pl.BlockSpec(memory_space=pltpu.SMEM)
LITTLE = pl.CostEstimate(flops=1, bytes_accessed=1, transcendentals=0)


def place_tiles(tile_set, slot_ids, slot_live, block_count):
    tile_edge = tile_set.shape[-1]
    onehot = (
        (slot_ids[:, None] == jnp.arange(3 * block_count, dtype=jnp.int32)[None, :])
        & slot_live[:, None]
    ).astype(jnp.bfloat16)
    dense_cols = jnp.einsum("sm,skn->mkn", onehot, tile_set, preferred_element_type=jnp.float32)
    return dense_cols.astype(jnp.bfloat16).reshape(3, block_count * tile_edge, tile_edge)


def gather_plan(tokens, cotangent, fwd_values, fwd_ids, fwd_count, bwd_ids, bwd_count):
    values = fwd_values[0]
    slot_ids = fwd_ids[0]
    slot_count = slot_ids.shape[0]
    tile_edge = values.shape[-1]
    whole_x, whole_dy = (
        lax.all_gather(tokens, "tensor", axis=1, tiled=True),
        lax.all_gather(cotangent, "tensor", axis=1, tiled=True),
    )
    row_count, feature_width = whole_x.shape
    block_count = feature_width // tile_edge
    slot_live = jnp.arange(slot_count, dtype=jnp.int32) < fwd_count[0]
    tile_kind = slot_ids // block_count
    tile_set = jnp.where((tile_kind == 2)[:, None, None], jnp.swapaxes(values, 1, 2), values)
    x_blocks_all = whole_x.reshape(row_count, block_count, tile_edge)
    dy_blocks_all = whole_dy.reshape(row_count, block_count, tile_edge)
    dense_cols = place_tiles(tile_set, slot_ids, slot_live, block_count)
    gate_pre = jnp.dot(whole_x, dense_cols[0], preferred_element_type=jnp.float32)
    up_val = jnp.dot(whole_x, dense_cols[1], preferred_element_type=jnp.float32)
    dhidden = jnp.dot(whole_dy, dense_cols[2], preferred_element_type=jnp.float32)
    hidden, dgate, up_grad = activations(gate_pre, up_val, dhidden)
    contract = (((1,), (1,)), ((), ()))
    dx_term = lax.dot_general(dgate, dense_cols[0], contract, preferred_element_type=jnp.float32)
    dx_term = dx_term + lax.dot_general(
        up_grad, dense_cols[1], contract, preferred_element_type=jnp.float32
    )
    input_grad = lax.psum_scatter(dx_term, "tensor", scatter_dimension=1, tiled=True).astype(
        jnp.bfloat16
    )
    back_ids = bwd_ids[0]
    back_count = back_ids.shape[0]
    back_live = jnp.arange(back_count, dtype=jnp.int32) < bwd_count[0]
    back_kind = back_ids // block_count
    back_block = back_ids % block_count
    tok_sel = jnp.take(x_blocks_all, back_block, axis=1)
    dy_sel = jnp.take(dy_blocks_all, back_block, axis=1)
    left_side = jnp.where((back_kind == 2)[None, :, None], hidden[:, None, :], tok_sel)
    right_side = jnp.where(
        (back_kind == 0)[None, :, None],
        dgate[:, None, :],
        jnp.where((back_kind == 1)[None, :, None], up_grad[:, None, :], dy_sel),
    )
    local_grad = jnp.einsum(
        "tbk,tbn->bkn", left_side, right_side, preferred_element_type=jnp.float32
    )
    local_grad = jnp.where(back_live[:, None, None], local_grad, jnp.float32(0.0))
    summed_grad = lax.psum(local_grad.astype(jnp.bfloat16), "dp")
    return (input_grad, summed_grad[None])


def activations(gate, up, dhidden):
    sig = jax.nn.sigmoid(gate)
    act = gate * sig
    hidden = (act * up).astype(BF)
    dgate = (dhidden * up * sig * (1.0 + gate * (1.0 - sig))).astype(BF)
    dup = (dhidden * act).astype(BF)
    return hidden, dgate, dup


def split(value, size):
    if size & (size - 1) == 0:
        return value >> (size.bit_length() - 1), value & (size - 1)
    return lax.div(value, size), lax.rem(value, size)


def spot_of(block, here_ref, n, per):
    shard, inner = split(block, per)
    up, odd = split(shard, 2)
    at = jnp.where(odd == 1, n - 1 - up, up)
    _, dist = split((here_ref[0] - at) * here_ref[1] + n, n)
    return dist * per + inner


def place_kernel(here_ref, ids_ref, cnt_ref, val_ref, gu_ref, d_ref, *, n, blocks, edge):
    gu_ref[...] = jnp.zeros_like(gu_ref)
    d_ref[...] = jnp.zeros_like(d_ref)

    def step(s, carry):
        e = ids_ref[s]
        kind, block = split(e, blocks)
        row = pl.multiple_of(spot_of(block, here_ref, n, blocks // n) * edge, edge)
        tile = val_ref[s]

        @pl.when(kind == 0)
        def _():
            gu_ref[pl.ds(row, edge), 0:edge] = tile

        @pl.when(kind == 1)
        def _():
            gu_ref[pl.ds(row, edge), edge : 2 * edge] = tile

        @pl.when(kind == 2)
        def _():
            d_ref[pl.ds(row, edge), :] = tile.T

        return carry

    lax.fori_loop(0, cnt_ref[0], step, 0)


def place(here, ids, count, values, n, blocks):
    edge = values.shape[-1]
    width = blocks * edge
    return pl.pallas_call(
        functools.partial(place_kernel, n=n, blocks=blocks, edge=edge),
        in_specs=[SMEM, SMEM, SMEM, VMEM],
        out_specs=[VMEM, VMEM],
        out_shape=[
            jax.ShapeDtypeStruct((width, 2 * edge), BF),
            jax.ShapeDtypeStruct((width, edge), BF),
        ],
        compiler_params=pltpu.CompilerParams(vmem_limit_bytes=24 * MIB),
        cost_estimate=LITTLE,
        name="place_weights",
    )(here, ids, count, values)


def forward_kernel(*refs, half, width):
    refs = list(refs)
    take = lambda k: [refs.pop(0) for _ in range(k)]
    x_m, y_m, x_s, y_s = take(half), take(half), take(half - 1), take(half - 1)
    w_gu, w_d, gu_m, dh_m, gu_s, dh_s = refs

    def total(parts, w, first):
        out = None
        for d, part in enumerate(parts, first):
            rows = w[d * width : (d + 1) * width, :]
            term = jnp.dot(part[...], rows, preferred_element_type=F32)
            out = term if out is None else out + term
        return out

    gu_m[...] = total(x_m, w_gu, 0)
    dh_m[...] = total(y_m, w_d, 0)
    gu_s[...] = total(x_s, w_gu, 1)
    dh_s[...] = total(y_s, w_d, 1)


def forward(x_m, y_m, x_s, y_s, w_gu, w_d):
    half = len(x_m)
    rows, width = x_m[0].shape
    edge = w_d.shape[1]
    gu, dh = (rows, 2 * edge), (rows, edge)
    arrays = [*x_m, *y_m, *x_s, *y_s, w_gu, w_d]
    return pl.pallas_call(
        functools.partial(forward_kernel, half=half, width=width),
        in_specs=[VMEM] * len(arrays),
        out_specs=[VMEM] * 4,
        out_shape=[jax.ShapeDtypeStruct(t, F32) for t in (gu, dh, gu, dh)],
        compiler_params=pltpu.CompilerParams(vmem_limit_bytes=28 * MIB),
        cost_estimate=LITTLE,
        name="forward_terms",
    )(*arrays)


def grads_kernel(here_ref, ids_ref, cnt_ref, *refs, half, blocks, edge):
    refs = list(refs)
    take = lambda k: [refs.pop(0) for _ in range(k)]
    x_m, y_m = take(half + 1), take(half + 1)
    x_s, y_s = take(half - 1), take(half - 1)
    dgu_m, dgu_s, hid_m, hid_s = take(4)
    out_ref, all_ref = refs[-2:]
    per = x_m[0].shape[1] // edge
    left = (((0,), (0,)), ((), ()))
    dot = lambda a, b: lax.dot_general(a, b, left, preferred_element_type=F32).astype(BF)
    both = lambda a, b: (a.astype(F32) + b.astype(F32)).astype(BF)
    hm, hs = hid_m[...], hid_s[...]

    for d in range(half + 1):
        base = d * per * 3
        pair = 0 < d < half
        for i in range(per):
            lane = slice(i * edge, (i + 1) * edge)
            g = dot(x_m[d][:, lane], dgu_m[...])
            h = dot(hm, y_m[d][:, lane])
            if pair:
                g = both(g, dot(x_s[d - 1][:, lane], dgu_s[...]))
                h = both(h, dot(hs, y_s[d - 1][:, lane]))
            all_ref[base + 3 * i] = g[:, :edge]
            all_ref[base + 3 * i + 1] = g[:, edge:]
            all_ref[base + 3 * i + 2] = h
    none = (half + 1) * per * 3
    all_ref[none] = jnp.zeros((edge, edge), BF)
    count = cnt_ref[0]

    def step(s, carry):
        e = ids_ref[s]
        kind, block = split(e, blocks)
        spot = spot_of(block, here_ref, 2 * half, per)
        held = (s < count) & (spot < (half + 1) * per)
        out_ref[s] = all_ref[jnp.where(held, spot * 3 + kind, none)]
        return carry

    lax.fori_loop(0, out_ref.shape[0], step, 0, unroll=4)


def tile_grads(here, ids, count, x_m, y_m, x_s, y_s, dgu_m, dgu_s, hid_m, hid_s, blocks):
    edge = hid_m.shape[1]
    half = len(x_m) - 1
    slots = ids.shape[0]
    tiles = (half + 1) * (x_m[0].shape[1] // edge) * 3 + 1
    arrays = [*x_m, *y_m, *x_s, *y_s, dgu_m, dgu_s, hid_m, hid_s]
    return pl.pallas_call(
        functools.partial(grads_kernel, half=half, blocks=blocks, edge=edge),
        in_specs=[SMEM, SMEM, SMEM] + [VMEM] * len(arrays),
        out_specs=VMEM,
        scratch_shapes=[pltpu.VMEM((tiles, edge, edge), BF)],
        out_shape=jax.ShapeDtypeStruct((slots, edge, edge), BF),
        compiler_params=pltpu.CompilerParams(vmem_limit_bytes=28 * MIB),
        cost_estimate=LITTLE,
        name="tile_gradients",
    )(here, ids, count, *arrays)


def sum_kernel(a_ref, b_ref, out_ref):
    size = out_ref.shape[0]
    rows = pl.ds(pl.program_id(0) * size, size)
    out_ref[...] = (a_ref[rows].astype(F32) + b_ref[rows].astype(F32)).astype(BF)


def sum_grads(a, b):
    slots, edge, _ = a.shape
    size = slots // 2 if slots % 2 == 0 else slots
    return pl.pallas_call(
        sum_kernel,
        grid=(slots // size,),
        in_specs=[pl.BlockSpec(memory_space=pltpu.VMEM)] * 2,
        out_specs=pl.BlockSpec((size, edge, edge), lambda i: (i, 0, 0)),
        out_shape=jax.ShapeDtypeStruct(a.shape, BF),
        compiler_params=pltpu.CompilerParams(vmem_limit_bytes=16 * MIB),
        cost_estimate=LITTLE,
        name="sum_tile_gradients",
    )(a, b)


def ring_plan(tokens, cotangent, fwd_values, fwd_ids, fwd_count, bwd_ids, bwd_count, *, n):
    half = n // 2
    ring = [2 * i for i in range(half)] + [2 * i + 1 for i in reversed(range(half))]
    perm, cross = [], []
    for i in range(n):
        ahead, behind = ring[(i + 1) % n], ring[(i - 1) % n]
        perm += [(ring[i] * 2, ahead * 2), (ring[i] * 2 + 1, behind * 2 + 1)]
        cross += [(ring[i] * 2 + 1, ahead * 2), (ring[i] * 2, behind * 2 + 1)]
    axes = ("tensor", "dp")
    hop = lambda v: lax.ppermute(v, axes, perm)
    swap = lambda v: lax.ppermute(v, "dp", [(0, 1), (1, 0)])

    values = fwd_values[0]
    edge = values.shape[-1]
    width = tokens.shape[1]
    blocks = n * (width // edge)

    shard = lax.axis_index("tensor")
    here = jnp.stack(
        [
            jnp.where(shard % 2 == 1, n - 1 - shard // 2, shard // 2),
            1 - 2 * lax.axis_index("dp"),
        ]
    ).astype(jnp.int32)
    w_gu, w_d = place(here, fwd_ids[0], fwd_count, values, n, blocks)

    x_m, y_m = [tokens, hop(tokens)], [cotangent, hop(cotangent)]
    x_s, y_s = [lax.ppermute(tokens, axes, cross)], [lax.ppermute(cotangent, axes, cross)]
    x_m[1], w_gu, w_d = lax.optimization_barrier((x_m[1], w_gu, w_d))
    for k in range(2, half + 1):
        x_m.append(hop(x_m[-1]))
        y_m.append(hop(y_m[-1]))
        if k < half:
            x_s.append(hop(x_s[-1]))
            y_s.append(hop(y_s[-1]))

    gu_m, dh_m, gu_s, dh_s = forward(x_m[:half], y_m[:half], x_s, y_s, w_gu, w_d)
    last = slice(half * width, (half + 1) * width)
    gu_m = gu_m + jnp.dot(x_m[half], w_gu[last], preferred_element_type=F32)
    dh_m = dh_m + jnp.dot(y_m[half], w_d[last], preferred_element_type=F32)
    gu_tm, dh_tm = gu_m + swap(gu_s), dh_m + swap(dh_s)
    gu_ts, dh_ts = gu_s + swap(gu_m), dh_s + swap(dh_m)

    hid_m, dg_m, du_m = activations(gu_tm[:, :edge], gu_tm[:, edge:], dh_tm)
    hid_s, dg_s, du_s = activations(gu_ts[:, :edge], gu_ts[:, edge:], dh_ts)
    dgu_m = jnp.concatenate([dg_m, du_m], axis=1)
    dgu_s = jnp.concatenate([dg_s, du_s], axis=1)

    def term(dgu, d):
        rows = w_gu[d * width : (d + 1) * width]
        return lax.dot_general(dgu, rows, (((1,), (1,)), ((), ())), preferred_element_type=F32)

    run_m = hop(term(dgu_m, half).astype(BF))
    run_s = hop(term(dgu_s, half + 1).astype(BF))
    grads = tile_grads(
        here, bwd_ids[0], bwd_count, x_m, y_m, x_s, y_s, dgu_m, dgu_s, hid_m, hid_s, blocks
    )
    run_m, grads = lax.optimization_barrier((run_m, grads))
    other = swap(grads)
    for d in range(half + 1, n):
        if d > half + 1:
            run_s = hop((term(dgu_s, d) + run_s.astype(F32)).astype(BF))
        run_m = hop((term(dgu_m, d) + run_m.astype(F32)).astype(BF))
    back = swap(run_s)

    grads = sum_grads(grads, other)
    run_m, grads = lax.optimization_barrier((run_m, grads))
    dx = term(dgu_m, 0) + run_m.astype(F32) + back.astype(F32)
    return dx.astype(BF), grads[None]


def on_device(tokens, cotangent, fwd_values, *rest, n, cores):
    width, edge = tokens.shape[1], fwd_values.shape[-1]
    if cores == 2 and n % 2 == 0 and 4 <= n <= 16 and width % edge == 0:
        return ring_plan(tokens, cotangent, fwd_values, *rest, n=n)
    return gather_plan(tokens, cotangent, fwd_values, *rest)


def solution(mesh):
    return jax.shard_map(
        functools.partial(on_device, n=mesh.shape["tensor"], cores=mesh.shape["dp"]),
        mesh=mesh,
        in_specs=(
            P(("groups", "dp"), "tensor"),
            P(("groups", "dp"), "tensor"),
            P(("groups", "tensor"), None, None, None),
            P(("groups", "tensor"), None),
            P(("groups", "tensor")),
            P(("groups", "tensor"), None),
            P(("groups", "tensor")),
        ),
        out_specs=(P(("groups", "dp"), "tensor"), P(("groups", "tensor"), None, None, None)),
        check_vma=False,
    )
```

```python
import functools

import jax
import jax.numpy as jnp
from jax import lax
from jax.experimental import pallas as pl
from jax.experimental.pallas import tpu as pltpu
from jax.sharding import PartitionSpec as P

BF = jnp.bfloat16
F32 = jnp.float32
MIB = 1024 * 1024
VMEM = pl.BlockSpec(memory_space=pltpu.VMEM)
SMEM = pl.BlockSpec(memory_space=pltpu.SMEM)
LITTLE = pl.CostEstimate(flops=1, bytes_accessed=1, transcendentals=0)


def place_tiles(tile_set, slot_ids, slot_live, block_count):
    tile_edge = tile_set.shape[-1]
    onehot = (
        (slot_ids[:, None] == jnp.arange(3 * block_count, dtype=jnp.int32)[None, :])
        & slot_live[:, None]
    ).astype(jnp.bfloat16)
    dense_cols = jnp.einsum("sm,skn->mkn", onehot, tile_set, preferred_element_type=jnp.float32)
    return dense_cols.astype(jnp.bfloat16).reshape(3, block_count * tile_edge, tile_edge)


def gather_plan(tokens, cotangent, fwd_values, fwd_ids, fwd_count, bwd_ids, bwd_count):
    values = fwd_values[0]
    slot_ids = fwd_ids[0]
    slot_count = slot_ids.shape[0]
    tile_edge = values.shape[-1]
    whole_x, whole_dy = (
        lax.all_gather(tokens, "tensor", axis=1, tiled=True),
        lax.all_gather(cotangent, "tensor", axis=1, tiled=True),
    )
    row_count, feature_width = whole_x.shape
    block_count = feature_width // tile_edge
    slot_live = jnp.arange(slot_count, dtype=jnp.int32) < fwd_count[0]
    tile_kind = slot_ids // block_count
    tile_set = jnp.where((tile_kind == 2)[:, None, None], jnp.swapaxes(values, 1, 2), values)
    x_blocks_all = whole_x.reshape(row_count, block_count, tile_edge)
    dy_blocks_all = whole_dy.reshape(row_count, block_count, tile_edge)
    dense_cols = place_tiles(tile_set, slot_ids, slot_live, block_count)
    gate_pre = jnp.dot(whole_x, dense_cols[0], preferred_element_type=jnp.float32)
    up_val = jnp.dot(whole_x, dense_cols[1], preferred_element_type=jnp.float32)
    dhidden = jnp.dot(whole_dy, dense_cols[2], preferred_element_type=jnp.float32)
    hidden, dgate, up_grad = activations(gate_pre, up_val, dhidden)
    contract = (((1,), (1,)), ((), ()))
    dx_term = lax.dot_general(dgate, dense_cols[0], contract, preferred_element_type=jnp.float32)
    dx_term = dx_term + lax.dot_general(
        up_grad, dense_cols[1], contract, preferred_element_type=jnp.float32
    )
    input_grad = lax.psum_scatter(dx_term, "tensor", scatter_dimension=1, tiled=True).astype(
        jnp.bfloat16
    )
    back_ids = bwd_ids[0]
    back_count = back_ids.shape[0]
    back_live = jnp.arange(back_count, dtype=jnp.int32) < bwd_count[0]
    back_kind = back_ids // block_count
    back_block = back_ids % block_count
    tok_sel = jnp.take(x_blocks_all, back_block, axis=1)
    dy_sel = jnp.take(dy_blocks_all, back_block, axis=1)
    left_side = jnp.where((back_kind == 2)[None, :, None], hidden[:, None, :], tok_sel)
    right_side = jnp.where(
        (back_kind == 0)[None, :, None],
        dgate[:, None, :],
        jnp.where((back_kind == 1)[None, :, None], up_grad[:, None, :], dy_sel),
    )
    local_grad = jnp.einsum(
        "tbk,tbn->bkn", left_side, right_side, preferred_element_type=jnp.float32
    )
    local_grad = jnp.where(back_live[:, None, None], local_grad, jnp.float32(0.0))
    summed_grad = lax.psum(local_grad.astype(jnp.bfloat16), "dp")
    return (input_grad, summed_grad[None])


def activations(gate, up, dhidden):
    sig = jax.nn.sigmoid(gate)
    act = gate * sig
    hidden = (act * up).astype(BF)
    dgate = (dhidden * up * sig * (1.0 + gate * (1.0 - sig))).astype(BF)
    dup = (dhidden * act).astype(BF)
    return hidden, dgate, dup


def split(value, size):
    if size & (size - 1) == 0:
        return value >> (size.bit_length() - 1), value & (size - 1)
    return lax.div(value, size), lax.rem(value, size)


def spot_of(block, here_ref, n, per):
    shard, inner = split(block, per)
    up, odd = split(shard, 2)
    at = jnp.where(odd == 1, n - 1 - up, up)
    _, dist = split((here_ref[0] - at) * here_ref[1] + n, n)
    return dist * per + inner


def place_kernel(here_ref, ids_ref, cnt_ref, val_ref, gu_ref, d_ref, *, n, blocks, edge):
    gu_ref[...] = jnp.zeros_like(gu_ref)
    d_ref[...] = jnp.zeros_like(d_ref)

    def step(s, carry):
        e = ids_ref[s]
        kind, block = split(e, blocks)
        row = pl.multiple_of(spot_of(block, here_ref, n, blocks // n) * edge, edge)
        tile = val_ref[s]

        @pl.when(kind == 0)
        def _():
            gu_ref[pl.ds(row, edge), 0:edge] = tile

        @pl.when(kind == 1)
        def _():
            gu_ref[pl.ds(row, edge), edge : 2 * edge] = tile

        @pl.when(kind == 2)
        def _():
            d_ref[pl.ds(row, edge), :] = tile.T

        return carry

    lax.fori_loop(0, cnt_ref[0], step, 0)


def place(here, ids, count, values, n, blocks):
    edge = values.shape[-1]
    width = blocks * edge
    return pl.pallas_call(
        functools.partial(place_kernel, n=n, blocks=blocks, edge=edge),
        in_specs=[SMEM, SMEM, SMEM, VMEM],
        out_specs=[VMEM, VMEM],
        out_shape=[
            jax.ShapeDtypeStruct((width, 2 * edge), BF),
            jax.ShapeDtypeStruct((width, edge), BF),
        ],
        compiler_params=pltpu.CompilerParams(vmem_limit_bytes=24 * MIB),
        cost_estimate=LITTLE,
        name="place_weights",
    )(here, ids, count, values)


def forward_kernel(*refs, half, width):
    refs = list(refs)
    take = lambda k: [refs.pop(0) for _ in range(k)]
    x_m, y_m, x_s, y_s = take(half), take(half), take(half - 1), take(half - 1)
    w_gu, w_d, gu_m, dh_m, gu_s, dh_s = refs

    def total(parts, w, first):
        out = None
        for d, part in enumerate(parts, first):
            rows = w[d * width : (d + 1) * width, :]
            term = jnp.dot(part[...], rows, preferred_element_type=F32)
            out = term if out is None else out + term
        return out

    gu_m[...] = total(x_m, w_gu, 0)
    dh_m[...] = total(y_m, w_d, 0)
    gu_s[...] = total(x_s, w_gu, 1)
    dh_s[...] = total(y_s, w_d, 1)


def forward(x_m, y_m, x_s, y_s, w_gu, w_d):
    half = len(x_m)
    rows, width = x_m[0].shape
    edge = w_d.shape[1]
    gu, dh = (rows, 2 * edge), (rows, edge)
    arrays = [*x_m, *y_m, *x_s, *y_s, w_gu, w_d]
    return pl.pallas_call(
        functools.partial(forward_kernel, half=half, width=width),
        in_specs=[VMEM] * len(arrays),
        out_specs=[VMEM] * 4,
        out_shape=[jax.ShapeDtypeStruct(t, F32) for t in (gu, dh, gu, dh)],
        compiler_params=pltpu.CompilerParams(vmem_limit_bytes=28 * MIB),
        cost_estimate=LITTLE,
        name="forward_terms",
    )(*arrays)


def grads_kernel(here_ref, ids_ref, cnt_ref, *refs, half, blocks, edge):
    refs = list(refs)
    take = lambda k: [refs.pop(0) for _ in range(k)]
    x_m, y_m = take(half + 1), take(half + 1)
    x_s, y_s = take(half - 1), take(half - 1)
    dgu_m, dgu_s, hid_m, hid_s = take(4)
    out_ref, all_ref = refs[-2:]
    per = x_m[0].shape[1] // edge
    left = (((0,), (0,)), ((), ()))
    dot = lambda a, b: lax.dot_general(a, b, left, preferred_element_type=F32).astype(BF)
    both = lambda a, b: (a.astype(F32) + b.astype(F32)).astype(BF)
    hm, hs = hid_m[...], hid_s[...]

    for d in range(half + 1):
        base = d * per * 3
        pair = 0 < d < half
        for i in range(per):
            lane = slice(i * edge, (i + 1) * edge)
            g = dot(x_m[d][:, lane], dgu_m[...])
            h = dot(hm, y_m[d][:, lane])
            if pair:
                g = both(g, dot(x_s[d - 1][:, lane], dgu_s[...]))
                h = both(h, dot(hs, y_s[d - 1][:, lane]))
            all_ref[base + 3 * i] = g[:, :edge]
            all_ref[base + 3 * i + 1] = g[:, edge:]
            all_ref[base + 3 * i + 2] = h
    none = (half + 1) * per * 3
    all_ref[none] = jnp.zeros((edge, edge), BF)
    count = cnt_ref[0]

    def step(s, carry):
        e = ids_ref[s]
        kind, block = split(e, blocks)
        spot = spot_of(block, here_ref, 2 * half, per)
        held = (s < count) & (spot < (half + 1) * per)
        out_ref[s] = all_ref[jnp.where(held, spot * 3 + kind, none)]
        return carry

    lax.fori_loop(0, out_ref.shape[0], step, 0, unroll=4)


def tile_grads(here, ids, count, x_m, y_m, x_s, y_s, dgu_m, dgu_s, hid_m, hid_s, blocks):
    edge = hid_m.shape[1]
    half = len(x_m) - 1
    slots = ids.shape[0]
    tiles = (half + 1) * (x_m[0].shape[1] // edge) * 3 + 1
    arrays = [*x_m, *y_m, *x_s, *y_s, dgu_m, dgu_s, hid_m, hid_s]
    return pl.pallas_call(
        functools.partial(grads_kernel, half=half, blocks=blocks, edge=edge),
        in_specs=[SMEM, SMEM, SMEM] + [VMEM] * len(arrays),
        out_specs=VMEM,
        scratch_shapes=[pltpu.VMEM((tiles, edge, edge), BF)],
        out_shape=jax.ShapeDtypeStruct((slots, edge, edge), BF),
        compiler_params=pltpu.CompilerParams(vmem_limit_bytes=28 * MIB),
        cost_estimate=LITTLE,
        name="tile_gradients",
    )(here, ids, count, *arrays)


def sum_kernel(a_ref, b_ref, out_ref):
    size = out_ref.shape[0]
    rows = pl.ds(pl.program_id(0) * size, size)
    out_ref[...] = (a_ref[rows].astype(F32) + b_ref[rows].astype(F32)).astype(BF)


def sum_grads(a, b):
    slots, edge, _ = a.shape
    size = slots // 2 if slots % 2 == 0 else slots
    return pl.pallas_call(
        sum_kernel,
        grid=(slots // size,),
        in_specs=[pl.BlockSpec(memory_space=pltpu.VMEM)] * 2,
        out_specs=pl.BlockSpec((size, edge, edge), lambda i: (i, 0, 0)),
        out_shape=jax.ShapeDtypeStruct(a.shape, BF),
        compiler_params=pltpu.CompilerParams(vmem_limit_bytes=16 * MIB),
        cost_estimate=LITTLE,
        name="sum_tile_gradients",
    )(a, b)


def ring_plan(tokens, cotangent, fwd_values, fwd_ids, fwd_count, bwd_ids, bwd_count, *, n):
    half = n // 2
    ring = [2 * i for i in range(half)] + [2 * i + 1 for i in reversed(range(half))]
    perm, cross = [], []
    for i in range(n):
        ahead, behind = ring[(i + 1) % n], ring[(i - 1) % n]
        perm += [(ring[i] * 2, ahead * 2), (ring[i] * 2 + 1, behind * 2 + 1)]
        cross += [(ring[i] * 2 + 1, ahead * 2), (ring[i] * 2, behind * 2 + 1)]
    axes = ("tensor", "dp")
    hop = lambda v: lax.ppermute(v, axes, perm)
    swap = lambda v: lax.ppermute(v, "dp", [(0, 1), (1, 0)])

    values = fwd_values[0]
    edge = values.shape[-1]
    width = tokens.shape[1]
    blocks = n * (width // edge)

    shard = lax.axis_index("tensor")
    here = jnp.stack(
        [
            jnp.where(shard % 2 == 1, n - 1 - shard // 2, shard // 2),
            1 - 2 * lax.axis_index("dp"),
        ]
    ).astype(jnp.int32)
    w_gu, w_d = place(here, fwd_ids[0], fwd_count, values, n, blocks)

    x_m, y_m = [tokens, hop(tokens)], [cotangent, hop(cotangent)]
    x_s, y_s = [lax.ppermute(tokens, axes, cross)], [lax.ppermute(cotangent, axes, cross)]
    x_m[1], w_gu, w_d = lax.optimization_barrier((x_m[1], w_gu, w_d))
    for k in range(2, half + 1):
        x_m.append(hop(x_m[-1]))
        y_m.append(hop(y_m[-1]))
        if k < half:
            x_s.append(hop(x_s[-1]))
            y_s.append(hop(y_s[-1]))

    gu_m, dh_m, gu_s, dh_s = forward(x_m[:half], y_m[:half], x_s, y_s, w_gu, w_d)
    last = slice(half * width, (half + 1) * width)
    gu_m = gu_m + jnp.dot(x_m[half], w_gu[last], preferred_element_type=F32)
    dh_m = dh_m + jnp.dot(y_m[half], w_d[last], preferred_element_type=F32)
    gu_tm, dh_tm = gu_m + swap(gu_s), dh_m + swap(dh_s)
    gu_ts, dh_ts = gu_s + swap(gu_m), dh_s + swap(dh_m)

    hid_m, dg_m, du_m = activations(gu_tm[:, :edge], gu_tm[:, edge:], dh_tm)
    hid_s, dg_s, du_s = activations(gu_ts[:, :edge], gu_ts[:, edge:], dh_ts)
    dgu_m = jnp.concatenate([dg_m, du_m], axis=1)
    dgu_s = jnp.concatenate([dg_s, du_s], axis=1)

    def term(dgu, d):
        rows = w_gu[d * width : (d + 1) * width]
        return lax.dot_general(dgu, rows, (((1,), (1,)), ((), ())), preferred_element_type=F32)

    run_m = hop(term(dgu_m, half).astype(BF))
    run_s = hop(term(dgu_s, half + 1).astype(BF))
    grads = tile_grads(
        here, bwd_ids[0], bwd_count, x_m, y_m, x_s, y_s, dgu_m, dgu_s, hid_m, hid_s, blocks
    )
    run_m, grads = lax.optimization_barrier((run_m, grads))
    other = swap(grads)
    for d in range(half + 1, n):
        if d > half + 1:
            run_s = hop((term(dgu_s, d) + run_s.astype(F32)).astype(BF))
        if d == half + 2:
            own = term(dgu_m, 0)
            run_m, own = lax.optimization_barrier((run_m, own))
        run_m = hop((term(dgu_m, d) + run_m.astype(F32)).astype(BF))
    back = swap(run_s)

    grads = sum_grads(grads, other)
    run_m, grads = lax.optimization_barrier((run_m, grads))
    dx = own + run_m.astype(F32) + back.astype(F32)
    return dx.astype(BF), grads[None]


def on_device(tokens, cotangent, fwd_values, *rest, n, cores):
    width, edge = tokens.shape[1], fwd_values.shape[-1]
    if cores == 2 and n % 2 == 0 and 6 <= n <= 16 and width % edge == 0:
        return ring_plan(tokens, cotangent, fwd_values, *rest, n=n)
    return gather_plan(tokens, cotangent, fwd_values, *rest)


def solution(mesh):
    return jax.shard_map(
        functools.partial(on_device, n=mesh.shape["tensor"], cores=mesh.shape["dp"]),
        mesh=mesh,
        in_specs=(
            P(("groups", "dp"), "tensor"),
            P(("groups", "dp"), "tensor"),
            P(("groups", "tensor"), None, None, None),
            P(("groups", "tensor"), None),
            P(("groups", "tensor")),
            P(("groups", "tensor"), None),
            P(("groups", "tensor")),
        ),
        out_specs=(P(("groups", "dp"), "tensor"), P(("groups", "tensor"), None, None, None)),
        check_vma=False,
    )
```

```python
import functools

import jax
import jax.numpy as jnp
from jax import lax
from jax.experimental import pallas as pl
from jax.experimental.pallas import tpu as pltpu
from jax.sharding import PartitionSpec as P

BF = jnp.bfloat16
F32 = jnp.float32
MIB = 1024 * 1024
VMEM = pl.BlockSpec(memory_space=pltpu.VMEM)
SMEM = pl.BlockSpec(memory_space=pltpu.SMEM)
LITTLE = pl.CostEstimate(flops=1, bytes_accessed=1, transcendentals=0)


def place_tiles(tile_set, slot_ids, slot_live, block_count):
    tile_edge = tile_set.shape[-1]
    onehot = (
        (slot_ids[:, None] == jnp.arange(3 * block_count, dtype=jnp.int32)[None, :])
        & slot_live[:, None]
    ).astype(jnp.bfloat16)
    dense_cols = jnp.einsum("sm,skn->mkn", onehot, tile_set, preferred_element_type=jnp.float32)
    return dense_cols.astype(jnp.bfloat16).reshape(3, block_count * tile_edge, tile_edge)


def gather_plan(tokens, cotangent, fwd_values, fwd_ids, fwd_count, bwd_ids, bwd_count):
    values = fwd_values[0]
    slot_ids = fwd_ids[0]
    slot_count = slot_ids.shape[0]
    tile_edge = values.shape[-1]
    whole_x, whole_dy = (
        lax.all_gather(tokens, "tensor", axis=1, tiled=True),
        lax.all_gather(cotangent, "tensor", axis=1, tiled=True),
    )
    row_count, feature_width = whole_x.shape
    block_count = feature_width // tile_edge
    slot_live = jnp.arange(slot_count, dtype=jnp.int32) < fwd_count[0]
    tile_kind = slot_ids // block_count
    tile_set = jnp.where((tile_kind == 2)[:, None, None], jnp.swapaxes(values, 1, 2), values)
    x_blocks_all = whole_x.reshape(row_count, block_count, tile_edge)
    dy_blocks_all = whole_dy.reshape(row_count, block_count, tile_edge)
    dense_cols = place_tiles(tile_set, slot_ids, slot_live, block_count)
    gate_pre = jnp.dot(whole_x, dense_cols[0], preferred_element_type=jnp.float32)
    up_val = jnp.dot(whole_x, dense_cols[1], preferred_element_type=jnp.float32)
    dhidden = jnp.dot(whole_dy, dense_cols[2], preferred_element_type=jnp.float32)
    hidden, dgate, up_grad = activations(gate_pre, up_val, dhidden)
    contract = (((1,), (1,)), ((), ()))
    dx_term = lax.dot_general(dgate, dense_cols[0], contract, preferred_element_type=jnp.float32)
    dx_term = dx_term + lax.dot_general(
        up_grad, dense_cols[1], contract, preferred_element_type=jnp.float32
    )
    input_grad = lax.psum_scatter(dx_term, "tensor", scatter_dimension=1, tiled=True).astype(
        jnp.bfloat16
    )
    back_ids = bwd_ids[0]
    back_count = back_ids.shape[0]
    back_live = jnp.arange(back_count, dtype=jnp.int32) < bwd_count[0]
    back_kind = back_ids // block_count
    back_block = back_ids % block_count
    tok_sel = jnp.take(x_blocks_all, back_block, axis=1)
    dy_sel = jnp.take(dy_blocks_all, back_block, axis=1)
    left_side = jnp.where((back_kind == 2)[None, :, None], hidden[:, None, :], tok_sel)
    right_side = jnp.where(
        (back_kind == 0)[None, :, None],
        dgate[:, None, :],
        jnp.where((back_kind == 1)[None, :, None], up_grad[:, None, :], dy_sel),
    )
    local_grad = jnp.einsum(
        "tbk,tbn->bkn", left_side, right_side, preferred_element_type=jnp.float32
    )
    local_grad = jnp.where(back_live[:, None, None], local_grad, jnp.float32(0.0))
    summed_grad = lax.psum(local_grad.astype(jnp.bfloat16), "dp")
    return (input_grad, summed_grad[None])


def activations(gate, up, dhidden):
    sig = jax.nn.sigmoid(gate)
    act = gate * sig
    hidden = (act * up).astype(BF)
    dgate = (dhidden * up * sig * (1.0 + gate * (1.0 - sig))).astype(BF)
    dup = (dhidden * act).astype(BF)
    return hidden, dgate, dup


def split(value, size):
    if size & (size - 1) == 0:
        return value >> (size.bit_length() - 1), value & (size - 1)
    return lax.div(value, size), lax.rem(value, size)


def spot_of(block, here_ref, n, per):
    shard, inner = split(block, per)
    up, odd = split(shard, 2)
    at = jnp.where(odd == 1, n - 1 - up, up)
    _, dist = split((here_ref[0] - at) * here_ref[1] + n, n)
    return dist * per + inner


def place_kernel(here_ref, ids_ref, cnt_ref, val_ref, gu_ref, d_ref, *, n, blocks, edge):
    gu_ref[...] = jnp.zeros_like(gu_ref)
    d_ref[...] = jnp.zeros_like(d_ref)

    def step(s, carry):
        e = ids_ref[s]
        kind, block = split(e, blocks)
        row = pl.multiple_of(spot_of(block, here_ref, n, blocks // n) * edge, edge)
        tile = val_ref[s]

        @pl.when(kind == 0)
        def _():
            gu_ref[pl.ds(row, edge), 0:edge] = tile

        @pl.when(kind == 1)
        def _():
            gu_ref[pl.ds(row, edge), edge : 2 * edge] = tile

        @pl.when(kind == 2)
        def _():
            d_ref[pl.ds(row, edge), :] = tile.T

        return carry

    lax.fori_loop(0, cnt_ref[0], step, 0)


def place(here, ids, count, values, n, blocks):
    edge = values.shape[-1]
    width = blocks * edge
    return pl.pallas_call(
        functools.partial(place_kernel, n=n, blocks=blocks, edge=edge),
        in_specs=[SMEM, SMEM, SMEM, VMEM],
        out_specs=[VMEM, VMEM],
        out_shape=[
            jax.ShapeDtypeStruct((width, 2 * edge), BF),
            jax.ShapeDtypeStruct((width, edge), BF),
        ],
        compiler_params=pltpu.CompilerParams(vmem_limit_bytes=24 * MIB),
        cost_estimate=LITTLE,
        name="place_weights",
    )(here, ids, count, values)


def forward_kernel(*refs, half, width):
    refs = list(refs)
    take = lambda k: [refs.pop(0) for _ in range(k)]
    x_m, y_m, x_s, y_s = take(half), take(half), take(half - 1), take(half - 1)
    w_gu, w_d, gu_m, dh_m, gu_s, dh_s = refs

    def total(parts, w, first):
        out = None
        for d, part in enumerate(parts, first):
            rows = w[d * width : (d + 1) * width, :]
            term = jnp.dot(part[...], rows, preferred_element_type=F32)
            out = term if out is None else out + term
        return out

    gu_m[...] = total(x_m, w_gu, 0)
    dh_m[...] = total(y_m, w_d, 0)
    gu_s[...] = total(x_s, w_gu, 1)
    dh_s[...] = total(y_s, w_d, 1)


def forward(x_m, y_m, x_s, y_s, w_gu, w_d):
    half = len(x_m)
    rows, width = x_m[0].shape
    edge = w_d.shape[1]
    gu, dh = (rows, 2 * edge), (rows, edge)
    arrays = [*x_m, *y_m, *x_s, *y_s, w_gu, w_d]
    return pl.pallas_call(
        functools.partial(forward_kernel, half=half, width=width),
        in_specs=[VMEM] * len(arrays),
        out_specs=[VMEM] * 4,
        out_shape=[jax.ShapeDtypeStruct(t, F32) for t in (gu, dh, gu, dh)],
        compiler_params=pltpu.CompilerParams(vmem_limit_bytes=28 * MIB),
        cost_estimate=LITTLE,
        name="forward_terms",
    )(*arrays)


def grads_kernel(here_ref, ids_ref, cnt_ref, *refs, half, blocks, edge):
    refs = list(refs)
    take = lambda k: [refs.pop(0) for _ in range(k)]
    x_m, y_m = take(half + 1), take(half + 1)
    x_s, y_s = take(half - 1), take(half - 1)
    dgu_m, dgu_s, hid_m, hid_s = take(4)
    out_ref, all_ref = refs[-2:]
    per = x_m[0].shape[1] // edge
    left = (((0,), (0,)), ((), ()))
    dot = lambda a, b: lax.dot_general(a, b, left, preferred_element_type=F32).astype(BF)
    both = lambda a, b: (a.astype(F32) + b.astype(F32)).astype(BF)
    hm, hs = hid_m[...], hid_s[...]

    for d in range(half + 1):
        base = d * per * 3
        pair = 0 < d < half
        for i in range(per):
            lane = slice(i * edge, (i + 1) * edge)
            g = dot(x_m[d][:, lane], dgu_m[...])
            h = dot(hm, y_m[d][:, lane])
            if pair:
                g = both(g, dot(x_s[d - 1][:, lane], dgu_s[...]))
                h = both(h, dot(hs, y_s[d - 1][:, lane]))
            all_ref[base + 3 * i] = g[:, :edge]
            all_ref[base + 3 * i + 1] = g[:, edge:]
            all_ref[base + 3 * i + 2] = h
    none = (half + 1) * per * 3
    all_ref[none] = jnp.zeros((edge, edge), BF)
    count = cnt_ref[0]

    def step(s, carry):
        e = ids_ref[s]
        kind, block = split(e, blocks)
        spot = spot_of(block, here_ref, 2 * half, per)
        held = (s < count) & (spot < (half + 1) * per)
        out_ref[s] = all_ref[jnp.where(held, spot * 3 + kind, none)]
        return carry

    lax.fori_loop(0, out_ref.shape[0], step, 0, unroll=4)


def tile_grads(here, ids, count, x_m, y_m, x_s, y_s, dgu_m, dgu_s, hid_m, hid_s, blocks):
    edge = hid_m.shape[1]
    half = len(x_m) - 1
    slots = ids.shape[0]
    tiles = (half + 1) * (x_m[0].shape[1] // edge) * 3 + 1
    arrays = [*x_m, *y_m, *x_s, *y_s, dgu_m, dgu_s, hid_m, hid_s]
    return pl.pallas_call(
        functools.partial(grads_kernel, half=half, blocks=blocks, edge=edge),
        in_specs=[SMEM, SMEM, SMEM] + [VMEM] * len(arrays),
        out_specs=VMEM,
        scratch_shapes=[pltpu.VMEM((tiles, edge, edge), BF)],
        out_shape=jax.ShapeDtypeStruct((slots, edge, edge), BF),
        compiler_params=pltpu.CompilerParams(vmem_limit_bytes=28 * MIB),
        cost_estimate=LITTLE,
        name="tile_gradients",
    )(here, ids, count, *arrays)


def sum_kernel(a_ref, b_ref, out_ref):
    size = out_ref.shape[0]
    rows = pl.ds(pl.program_id(0) * size, size)
    out_ref[...] = (a_ref[rows].astype(F32) + b_ref[rows].astype(F32)).astype(BF)


def sum_grads(a, b):
    slots, edge, _ = a.shape
    size = slots // 2 if slots % 2 == 0 else slots
    return pl.pallas_call(
        sum_kernel,
        grid=(slots // size,),
        in_specs=[pl.BlockSpec(memory_space=pltpu.VMEM)] * 2,
        out_specs=pl.BlockSpec((size, edge, edge), lambda i: (i, 0, 0)),
        out_shape=jax.ShapeDtypeStruct(a.shape, BF),
        compiler_params=pltpu.CompilerParams(vmem_limit_bytes=16 * MIB),
        cost_estimate=LITTLE,
        name="sum_tile_gradients",
    )(a, b)


def ring_plan(tokens, cotangent, fwd_values, fwd_ids, fwd_count, bwd_ids, bwd_count, *, n):
    half = n // 2
    ring = [2 * i for i in range(half)] + [2 * i + 1 for i in reversed(range(half))]
    perm, cross = [], []
    for i in range(n):
        ahead, behind = ring[(i + 1) % n], ring[(i - 1) % n]
        perm += [(ring[i] * 2, ahead * 2), (ring[i] * 2 + 1, behind * 2 + 1)]
        cross += [(ring[i] * 2 + 1, ahead * 2), (ring[i] * 2, behind * 2 + 1)]
    axes = ("tensor", "dp")
    hop = lambda v: lax.ppermute(v, axes, perm)
    swap = lambda v: lax.ppermute(v, "dp", [(0, 1), (1, 0)])

    values = fwd_values[0]
    edge = values.shape[-1]
    width = tokens.shape[1]
    blocks = n * (width // edge)

    shard = lax.axis_index("tensor")
    here = jnp.stack(
        [
            jnp.where(shard % 2 == 1, n - 1 - shard // 2, shard // 2),
            1 - 2 * lax.axis_index("dp"),
        ]
    ).astype(jnp.int32)
    w_gu, w_d = place(here, fwd_ids[0], fwd_count, values, n, blocks)

    x_m, y_m = [tokens, hop(tokens)], [cotangent, hop(cotangent)]
    x_s, y_s = [lax.ppermute(tokens, axes, cross)], [lax.ppermute(cotangent, axes, cross)]
    x_m[1], w_gu, w_d = lax.optimization_barrier((x_m[1], w_gu, w_d))
    for k in range(2, half + 1):
        x_m.append(hop(x_m[-1]))
        y_m.append(hop(y_m[-1]))
        if k < half:
            if k == half - 1:
                x_s[-1], _ = lax.optimization_barrier((x_s[-1], x_m[-1]))
                y_s[-1], _ = lax.optimization_barrier((y_s[-1], y_m[-1]))
            x_s.append(hop(x_s[-1]))
            y_s.append(hop(y_s[-1]))

    gu_m, dh_m, gu_s, dh_s = forward(x_m[:half], y_m[:half], x_s, y_s, w_gu, w_d)
    last = slice(half * width, (half + 1) * width)
    gu_m = gu_m + jnp.dot(x_m[half], w_gu[last], preferred_element_type=F32)
    dh_m = dh_m + jnp.dot(y_m[half], w_d[last], preferred_element_type=F32)
    gu_tm, dh_tm = gu_m + swap(gu_s), dh_m + swap(dh_s)
    gu_ts, dh_ts = gu_s + swap(gu_m), dh_s + swap(dh_m)

    hid_m, dg_m, du_m = activations(gu_tm[:, :edge], gu_tm[:, edge:], dh_tm)
    hid_s, dg_s, du_s = activations(gu_ts[:, :edge], gu_ts[:, edge:], dh_ts)
    dgu_m = jnp.concatenate([dg_m, du_m], axis=1)
    dgu_s = jnp.concatenate([dg_s, du_s], axis=1)

    def term(dgu, d):
        rows = w_gu[d * width : (d + 1) * width]
        return lax.dot_general(dgu, rows, (((1,), (1,)), ((), ())), preferred_element_type=F32)

    run_m = hop(term(dgu_m, half).astype(BF))
    run_s = hop(term(dgu_s, half + 1).astype(BF))
    grads = tile_grads(
        here, bwd_ids[0], bwd_count, x_m, y_m, x_s, y_s, dgu_m, dgu_s, hid_m, hid_s, blocks
    )
    run_m, grads = lax.optimization_barrier((run_m, grads))
    other = swap(grads)
    for d in range(half + 1, n):
        if d > half + 1:
            run_s = hop((term(dgu_s, d) + run_s.astype(F32)).astype(BF))
        if d == half + 2:
            own = term(dgu_m, 0)
            run_m, own = lax.optimization_barrier((run_m, own))
        run_m = hop((term(dgu_m, d) + run_m.astype(F32)).astype(BF))
    back = swap(run_s)

    grads = sum_grads(grads, other)
    run_m, grads = lax.optimization_barrier((run_m, grads))
    dx = own + run_m.astype(F32) + back.astype(F32)
    return dx.astype(BF), grads[None]


def on_device(tokens, cotangent, fwd_values, *rest, n, cores):
    width, edge = tokens.shape[1], fwd_values.shape[-1]
    if cores == 2 and n % 2 == 0 and 6 <= n <= 16 and width % edge == 0:
        return ring_plan(tokens, cotangent, fwd_values, *rest, n=n)
    return gather_plan(tokens, cotangent, fwd_values, *rest)


def solution(mesh):
    return jax.shard_map(
        functools.partial(on_device, n=mesh.shape["tensor"], cores=mesh.shape["dp"]),
        mesh=mesh,
        in_specs=(
            P(("groups", "dp"), "tensor"),
            P(("groups", "dp"), "tensor"),
            P(("groups", "tensor"), None, None, None),
            P(("groups", "tensor"), None),
            P(("groups", "tensor")),
            P(("groups", "tensor"), None),
            P(("groups", "tensor")),
        ),
        out_specs=(P(("groups", "dp"), "tensor"), P(("groups", "tensor"), None, None, None)),
        check_vma=False,
    )
```

```python
import functools

import jax
import jax.numpy as jnp
from jax import lax
from jax.experimental import pallas as pl
from jax.experimental.pallas import tpu as pltpu
from jax.sharding import PartitionSpec as P

BF = jnp.bfloat16
F32 = jnp.float32
MIB = 1024 * 1024
VMEM = pl.BlockSpec(memory_space=pltpu.VMEM)
SMEM = pl.BlockSpec(memory_space=pltpu.SMEM)
LITTLE = pl.CostEstimate(flops=1, bytes_accessed=1, transcendentals=0)


def place_tiles(tile_set, slot_ids, slot_live, block_count):
    tile_edge = tile_set.shape[-1]
    onehot = (
        (slot_ids[:, None] == jnp.arange(3 * block_count, dtype=jnp.int32)[None, :])
        & slot_live[:, None]
    ).astype(jnp.bfloat16)
    dense_cols = jnp.einsum("sm,skn->mkn", onehot, tile_set, preferred_element_type=jnp.float32)
    return dense_cols.astype(jnp.bfloat16).reshape(3, block_count * tile_edge, tile_edge)


def gather_plan(tokens, cotangent, fwd_values, fwd_ids, fwd_count, bwd_ids, bwd_count):
    values = fwd_values[0]
    slot_ids = fwd_ids[0]
    slot_count = slot_ids.shape[0]
    tile_edge = values.shape[-1]
    whole_x, whole_dy = (
        lax.all_gather(tokens, "tensor", axis=1, tiled=True),
        lax.all_gather(cotangent, "tensor", axis=1, tiled=True),
    )
    row_count, feature_width = whole_x.shape
    block_count = feature_width // tile_edge
    slot_live = jnp.arange(slot_count, dtype=jnp.int32) < fwd_count[0]
    tile_kind = slot_ids // block_count
    tile_set = jnp.where((tile_kind == 2)[:, None, None], jnp.swapaxes(values, 1, 2), values)
    x_blocks_all = whole_x.reshape(row_count, block_count, tile_edge)
    dy_blocks_all = whole_dy.reshape(row_count, block_count, tile_edge)
    dense_cols = place_tiles(tile_set, slot_ids, slot_live, block_count)
    gate_pre = jnp.dot(whole_x, dense_cols[0], preferred_element_type=jnp.float32)
    up_val = jnp.dot(whole_x, dense_cols[1], preferred_element_type=jnp.float32)
    dhidden = jnp.dot(whole_dy, dense_cols[2], preferred_element_type=jnp.float32)
    hidden, dgate, up_grad = activations(gate_pre, up_val, dhidden)
    contract = (((1,), (1,)), ((), ()))
    dx_term = lax.dot_general(dgate, dense_cols[0], contract, preferred_element_type=jnp.float32)
    dx_term = dx_term + lax.dot_general(
        up_grad, dense_cols[1], contract, preferred_element_type=jnp.float32
    )
    input_grad = lax.psum_scatter(dx_term, "tensor", scatter_dimension=1, tiled=True).astype(
        jnp.bfloat16
    )
    back_ids = bwd_ids[0]
    back_count = back_ids.shape[0]
    back_live = jnp.arange(back_count, dtype=jnp.int32) < bwd_count[0]
    back_kind = back_ids // block_count
    back_block = back_ids % block_count
    tok_sel = jnp.take(x_blocks_all, back_block, axis=1)
    dy_sel = jnp.take(dy_blocks_all, back_block, axis=1)
    left_side = jnp.where((back_kind == 2)[None, :, None], hidden[:, None, :], tok_sel)
    right_side = jnp.where(
        (back_kind == 0)[None, :, None],
        dgate[:, None, :],
        jnp.where((back_kind == 1)[None, :, None], up_grad[:, None, :], dy_sel),
    )
    local_grad = jnp.einsum(
        "tbk,tbn->bkn", left_side, right_side, preferred_element_type=jnp.float32
    )
    local_grad = jnp.where(back_live[:, None, None], local_grad, jnp.float32(0.0))
    summed_grad = lax.psum(local_grad.astype(jnp.bfloat16), "dp")
    return (input_grad, summed_grad[None])


def activations(gate, up, dhidden):
    sig = jax.nn.sigmoid(gate)
    act = gate * sig
    hidden = (act * up).astype(BF)
    dgate = (dhidden * up * sig * (1.0 + gate * (1.0 - sig))).astype(BF)
    dup = (dhidden * act).astype(BF)
    return hidden, dgate, dup


def split(value, size):
    if size & (size - 1) == 0:
        return value >> (size.bit_length() - 1), value & (size - 1)
    return lax.div(value, size), lax.rem(value, size)


def spot_of(block, here_ref, n, per):
    shard, inner = split(block, per)
    up, odd = split(shard, 2)
    at = jnp.where(odd == 1, n - 1 - up, up)
    _, dist = split((here_ref[0] - at) * here_ref[1] + n, n)
    return dist * per + inner


def place_kernel(here_ref, ids_ref, cnt_ref, val_ref, gu_ref, d_ref, *, n, blocks, edge):
    gu_ref[...] = jnp.zeros_like(gu_ref)
    d_ref[...] = jnp.zeros_like(d_ref)

    def step(s, carry):
        e = ids_ref[s]
        kind, block = split(e, blocks)
        row = pl.multiple_of(spot_of(block, here_ref, n, blocks // n) * edge, edge)
        tile = val_ref[s]

        @pl.when(kind == 0)
        def _():
            gu_ref[pl.ds(row, edge), 0:edge] = tile

        @pl.when(kind == 1)
        def _():
            gu_ref[pl.ds(row, edge), edge : 2 * edge] = tile

        @pl.when(kind == 2)
        def _():
            d_ref[pl.ds(row, edge), :] = tile.T

        return carry

    lax.fori_loop(0, cnt_ref[0], step, 0)


def place(here, ids, count, values, n, blocks):
    edge = values.shape[-1]
    width = blocks * edge
    return pl.pallas_call(
        functools.partial(place_kernel, n=n, blocks=blocks, edge=edge),
        in_specs=[SMEM, SMEM, SMEM, VMEM],
        out_specs=[VMEM, VMEM],
        out_shape=[
            jax.ShapeDtypeStruct((width, 2 * edge), BF),
            jax.ShapeDtypeStruct((width, edge), BF),
        ],
        compiler_params=pltpu.CompilerParams(vmem_limit_bytes=24 * MIB),
        cost_estimate=LITTLE,
        name="place_weights",
    )(here, ids, count, values)


def forward_kernel(*refs, half, width):
    refs = list(refs)
    take = lambda k: [refs.pop(0) for _ in range(k)]
    x_m, y_m, x_s, y_s = take(half), take(half), take(half - 1), take(half - 1)
    w_gu, w_d, gu_m, dh_m, gu_s, dh_s = refs

    def total(parts, w, first):
        out = None
        for d, part in enumerate(parts, first):
            rows = w[d * width : (d + 1) * width, :]
            term = jnp.dot(part[...], rows, preferred_element_type=F32)
            out = term if out is None else out + term
        return out

    gu_m[...] = total(x_m, w_gu, 0)
    dh_m[...] = total(y_m, w_d, 0)
    gu_s[...] = total(x_s, w_gu, 1)
    dh_s[...] = total(y_s, w_d, 1)


def forward(x_m, y_m, x_s, y_s, w_gu, w_d):
    half = len(x_m)
    rows, width = x_m[0].shape
    edge = w_d.shape[1]
    gu, dh = (rows, 2 * edge), (rows, edge)
    arrays = [*x_m, *y_m, *x_s, *y_s, w_gu, w_d]
    return pl.pallas_call(
        functools.partial(forward_kernel, half=half, width=width),
        in_specs=[VMEM] * len(arrays),
        out_specs=[VMEM] * 4,
        out_shape=[jax.ShapeDtypeStruct(t, F32) for t in (gu, dh, gu, dh)],
        compiler_params=pltpu.CompilerParams(vmem_limit_bytes=28 * MIB),
        cost_estimate=LITTLE,
        name="forward_terms",
    )(*arrays)


def grads_kernel(here_ref, ids_ref, cnt_ref, *refs, half, blocks, edge):
    refs = list(refs)
    take = lambda k: [refs.pop(0) for _ in range(k)]
    x_m, y_m = take(half + 1), take(half + 1)
    x_s, y_s = take(half - 1), take(half - 1)
    dgu_m, dgu_s, hid_m, hid_s = take(4)
    out_ref, all_ref = refs[-2:]
    per = x_m[0].shape[1] // edge
    left = (((0,), (0,)), ((), ()))
    dot = lambda a, b: lax.dot_general(a, b, left, preferred_element_type=F32).astype(BF)
    both = lambda a, b: (a.astype(F32) + b.astype(F32)).astype(BF)
    hm, hs = hid_m[...], hid_s[...]

    for d in range(half + 1):
        base = d * per * 3
        pair = 0 < d < half
        for i in range(per):
            lane = slice(i * edge, (i + 1) * edge)
            g = dot(x_m[d][:, lane], dgu_m[...])
            h = dot(hm, y_m[d][:, lane])
            if pair:
                g = both(g, dot(x_s[d - 1][:, lane], dgu_s[...]))
                h = both(h, dot(hs, y_s[d - 1][:, lane]))
            all_ref[base + 3 * i] = g[:, :edge]
            all_ref[base + 3 * i + 1] = g[:, edge:]
            all_ref[base + 3 * i + 2] = h
    none = (half + 1) * per * 3
    all_ref[none] = jnp.zeros((edge, edge), BF)
    count = cnt_ref[0]

    def step(s, carry):
        e = ids_ref[s]
        kind, block = split(e, blocks)
        spot = spot_of(block, here_ref, 2 * half, per)
        held = (s < count) & (spot < (half + 1) * per)
        out_ref[s] = all_ref[jnp.where(held, spot * 3 + kind, none)]
        return carry

    lax.fori_loop(0, out_ref.shape[0], step, 0, unroll=4)


def tile_grads(here, ids, count, x_m, y_m, x_s, y_s, dgu_m, dgu_s, hid_m, hid_s, blocks):
    edge = hid_m.shape[1]
    half = len(x_m) - 1
    slots = ids.shape[0]
    tiles = (half + 1) * (x_m[0].shape[1] // edge) * 3 + 1
    arrays = [*x_m, *y_m, *x_s, *y_s, dgu_m, dgu_s, hid_m, hid_s]
    return pl.pallas_call(
        functools.partial(grads_kernel, half=half, blocks=blocks, edge=edge),
        in_specs=[SMEM, SMEM, SMEM] + [VMEM] * len(arrays),
        out_specs=VMEM,
        scratch_shapes=[pltpu.VMEM((tiles, edge, edge), BF)],
        out_shape=jax.ShapeDtypeStruct((slots, edge, edge), BF),
        compiler_params=pltpu.CompilerParams(vmem_limit_bytes=28 * MIB),
        cost_estimate=LITTLE,
        name="tile_gradients",
    )(here, ids, count, *arrays)


def sum_kernel(a_ref, b_ref, out_ref):
    size = out_ref.shape[0]
    rows = pl.ds(pl.program_id(0) * size, size)
    out_ref[...] = (a_ref[rows].astype(F32) + b_ref[rows].astype(F32)).astype(BF)


def sum_grads(a, b):
    slots, edge, _ = a.shape
    size = slots // 2 if slots % 2 == 0 else slots
    return pl.pallas_call(
        sum_kernel,
        grid=(slots // size,),
        in_specs=[pl.BlockSpec(memory_space=pltpu.VMEM)] * 2,
        out_specs=pl.BlockSpec((size, edge, edge), lambda i: (i, 0, 0)),
        out_shape=jax.ShapeDtypeStruct(a.shape, BF),
        compiler_params=pltpu.CompilerParams(vmem_limit_bytes=16 * MIB),
        cost_estimate=LITTLE,
        name="sum_tile_gradients",
    )(a, b)


def ring_plan(tokens, cotangent, fwd_values, fwd_ids, fwd_count, bwd_ids, bwd_count, *, n):
    half = n // 2
    ring = [2 * i for i in range(half)] + [2 * i + 1 for i in reversed(range(half))]
    perm, cross = [], []
    for i in range(n):
        ahead, behind = ring[(i + 1) % n], ring[(i - 1) % n]
        perm += [(ring[i] * 2, ahead * 2), (ring[i] * 2 + 1, behind * 2 + 1)]
        cross += [(ring[i] * 2 + 1, ahead * 2), (ring[i] * 2, behind * 2 + 1)]
    axes = ("tensor", "dp")
    hop = lambda v: lax.ppermute(v, axes, perm)
    swap = lambda v: lax.ppermute(v, "dp", [(0, 1), (1, 0)])

    values = fwd_values[0]
    edge = values.shape[-1]
    width = tokens.shape[1]
    blocks = n * (width // edge)

    shard = lax.axis_index("tensor")
    here = jnp.stack(
        [
            jnp.where(shard % 2 == 1, n - 1 - shard // 2, shard // 2),
            1 - 2 * lax.axis_index("dp"),
        ]
    ).astype(jnp.int32)
    w_gu, w_d = place(here, fwd_ids[0], fwd_count, values, n, blocks)

    x_m, y_m = [tokens, hop(tokens)], [cotangent, hop(cotangent)]
    x_s, y_s = [lax.ppermute(tokens, axes, cross)], [lax.ppermute(cotangent, axes, cross)]
    x_m[1], w_gu, w_d = lax.optimization_barrier((x_m[1], w_gu, w_d))
    for k in range(2, half + 1):
        x_m.append(hop(x_m[-1]))
        y_m.append(hop(y_m[-1]))
        if k < half:
            x_s[-1], _ = lax.optimization_barrier((x_s[-1], x_m[-1]))
            y_s[-1], _ = lax.optimization_barrier((y_s[-1], y_m[-1]))
            x_s.append(hop(x_s[-1]))
            y_s.append(hop(y_s[-1]))

    gu_m, dh_m, gu_s, dh_s = forward(x_m[:half], y_m[:half], x_s, y_s, w_gu, w_d)
    last = slice(half * width, (half + 1) * width)
    gu_m = gu_m + jnp.dot(x_m[half], w_gu[last], preferred_element_type=F32)
    dh_m = dh_m + jnp.dot(y_m[half], w_d[last], preferred_element_type=F32)
    gu_tm, dh_tm = gu_m + swap(gu_s), dh_m + swap(dh_s)
    gu_ts, dh_ts = gu_s + swap(gu_m), dh_s + swap(dh_m)

    hid_m, dg_m, du_m = activations(gu_tm[:, :edge], gu_tm[:, edge:], dh_tm)
    hid_s, dg_s, du_s = activations(gu_ts[:, :edge], gu_ts[:, edge:], dh_ts)
    dgu_m = jnp.concatenate([dg_m, du_m], axis=1)
    dgu_s = jnp.concatenate([dg_s, du_s], axis=1)

    def term(dgu, d):
        rows = w_gu[d * width : (d + 1) * width]
        return lax.dot_general(dgu, rows, (((1,), (1,)), ((), ())), preferred_element_type=F32)

    run_m = hop(term(dgu_m, half).astype(BF))
    run_s = hop(term(dgu_s, half + 1).astype(BF))
    grads = tile_grads(
        here, bwd_ids[0], bwd_count, x_m, y_m, x_s, y_s, dgu_m, dgu_s, hid_m, hid_s, blocks
    )
    run_m, grads = lax.optimization_barrier((run_m, grads))
    other = swap(grads)
    for d in range(half + 1, n):
        if d > half + 1:
            run_s = hop((term(dgu_s, d) + run_s.astype(F32)).astype(BF))
        if d == half + 2:
            own = term(dgu_m, 0)
            run_m, own = lax.optimization_barrier((run_m, own))
        run_m = hop((term(dgu_m, d) + run_m.astype(F32)).astype(BF))
    back = swap(run_s)

    grads = sum_grads(grads, other)
    run_m, grads = lax.optimization_barrier((run_m, grads))
    dx = own + run_m.astype(F32) + back.astype(F32)
    return dx.astype(BF), grads[None]


def on_device(tokens, cotangent, fwd_values, *rest, n, cores):
    width, edge = tokens.shape[1], fwd_values.shape[-1]
    if cores == 2 and n % 2 == 0 and 6 <= n <= 16 and width % edge == 0:
        return ring_plan(tokens, cotangent, fwd_values, *rest, n=n)
    return gather_plan(tokens, cotangent, fwd_values, *rest)


def solution(mesh):
    return jax.shard_map(
        functools.partial(on_device, n=mesh.shape["tensor"], cores=mesh.shape["dp"]),
        mesh=mesh,
        in_specs=(
            P(("groups", "dp"), "tensor"),
            P(("groups", "dp"), "tensor"),
            P(("groups", "tensor"), None, None, None),
            P(("groups", "tensor"), None),
            P(("groups", "tensor")),
            P(("groups", "tensor"), None),
            P(("groups", "tensor")),
        ),
        out_specs=(P(("groups", "dp"), "tensor"), P(("groups", "tensor"), None, None, None)),
        check_vma=False,
    )
```
